32 devices in a mesh: dp: 8 (over z, x), section: 4 (over y, core).
Axes of the slice: x: 2, y: 2, z: 4, core: 2. Of those that a mesh axis runs over, the one named last changes fastest.
Arguments:
- images_in: bfloat16 [2048, 4096], P(('dp', 'section')), may hold values from -6 to 6
- labels: int32 [2048], P(('dp', 'section')), may hold values from 0 to 9
- conv_weight: float32 [3, 2, 576, 64], P(None, None, None, 'section'), may hold values from -0.25 to 0.25
- frn_gain: float32 [3, 2, 64], replicated, may hold values from 0.25 to 1.75
- frn_bias: float32 [3, 2, 64], replicated, may hold values from -3 to 3
- head_weight: float32 [64, 10], replicated, as said below
- head_bias: float32 [10], replicated, may hold values from -4 to 4
Outputs:
- grad_conv: float32 [3, 2, 576, 64], P(None, None, None, 'section')
- grad_norm: float32 [3, 2, 2, 64], replicated
- grad_head_weight: float32 [64, 10], replicated
- grad_head_bias: float32 [10], replicated
The draws below stay inside these ranges and needn't reach their ends.
Inputs may be any that keep to these rules, and one draw needn't show every extreme that they name: `head_weight`: the classifier's weights.
All inputs are finite; a program needn't handle non-finite values.
Results may differ from the reference program's by a relative error of at most 0.0033.
The reference program's roundings to bfloat16 on the way count: a program that leaves them out, or rounds other values in their place, can miss the bound.
Values may be sent and summed in bfloat16 or wider, within the bound.
A program may use at most 64 MiB of HBM per device.

```python
import math
import jax
import jax.numpy as jnp
from jax import lax

C = 64
CLASSES = 10
BLOCKS = 3
SIDE = 8
MICRO = 8
IMG_DEV = 64
PIX = 64
IMAGES = 2048


def draw_head_weight(key, part):
    first = jax.random.fold_in(key, 0)
    base = jnp.clip(jax.random.normal(first, (C, CLASSES), jnp.float32), -4.0, 4.0)
    return base * (2.5 / math.sqrt(C))


def touch_ends(array, own_key, smallest, largest):
    place = [jax.random.randint(jax.random.fold_in(own_key, axis), (), 0, length) for axis, length in enumerate(array.shape)]
    widest = array.shape.index(max(array.shape))
    beside = place[:widest] + [(place[widest] + 1) % array.shape[widest]] + place[widest + 1:]
    return array.at[tuple(place)].set(smallest).at[tuple(beside)].set(largest)


def block_levels(key, shape, shards, least, largest):
    level = 1.0
    for dim, shards_of in shards:
        steps = jax.random.uniform(jax.random.fold_in(jax.random.fold_in(key, 6), dim), (shards_of,), jnp.float32, least / len(shards), largest / len(shards))
        level = level * jnp.repeat(jnp.exp(steps), shape[dim] // shards_of).reshape((-1,) + (1,) * (len(shape) - 1 - dim))
    return level


def scatter_about(rng, dims, scale, bound, cuts=(), held_as=jnp.bfloat16):
    values = jax.random.normal(rng, dims, jnp.float32) * scale
    if len(cuts) > 0:
        values = block_levels(rng, dims, cuts, -0.22, 0.18) * values
    return jnp.clip(values, min=-bound, max=bound).astype(held_as)


def setup_inputs(seed: int = 0) -> dict:
    arg_keys = jax.random.split(jax.random.key(seed), 8)
    return {
        "images_in": scatter_about(arg_keys[0], (IMAGES, PIX * C), 1.0, 6.0, ((0, 32),)),
        "labels": touch_ends(jax.random.randint(arg_keys[1], (IMAGES,), 0, CLASSES), jax.random.fold_in(arg_keys[1], 1), 0, CLASSES - 1).astype(jnp.int32),
        "conv_weight": scatter_about(arg_keys[2], (BLOCKS, 2, 9 * C, C), (9 * C) ** -0.5, 0.25, ((3, 4),), jnp.float32),
        "frn_gain": jnp.clip(1.0 + 0.15 * jax.random.normal(arg_keys[3], (BLOCKS, 2, C), jnp.float32), 0.25, 1.75),
        "frn_bias": scatter_about(arg_keys[4], (BLOCKS, 2, C), 0.5, 3.0, (), jnp.float32),
        "head_weight": draw_head_weight(jax.random.fold_in(arg_keys[7], 71), 0),
        "head_bias": scatter_about(arg_keys[6], (CLASSES,), 1.0, 4.0, (), jnp.float32),
    }


eps = 1e-06
prior_precision = 0.5

def make_patches(maps):
    side = maps.shape[1]
    padded = jnp.pad(maps, ((0, 0), (1, 1), (1, 1), (0, 0)))
    taps = [padded[:, a:a + side, e:e + side, :] for a in range(3) for e in range(3)]
    stacked = jnp.concatenate(taps, axis=3)
    return stacked.reshape(maps.shape[0] * side * side, 9 * maps.shape[3])

def fold_patches(columns, shape):
    back = jax.vjp(make_patches, jnp.zeros(shape, jnp.float32))[1]
    return back(columns)[0]

def respond(values, gain, bias, count):
    grouped = values.reshape(count, -1, values.shape[1])
    energy = lax.optimization_barrier(jnp.mean(grouped * grouped, axis=1, keepdims=True))
    normed = grouped * lax.rsqrt(energy + eps)
    return (gain * normed + bias).reshape(values.shape)

def swish(values):
    return values * jax.nn.sigmoid(values)

def block_forward(maps, weights, gains, biases):
    count = maps.shape[0]
    w_first = weights[0].astype(jnp.bfloat16)
    w_second = weights[1].astype(jnp.bfloat16)
    cols_first = make_patches(maps)
    pre_first = jnp.dot(cols_first, w_first, preferred_element_type=jnp.float32)
    hidden = swish(respond(pre_first, gains[0], biases[0], count)).astype(jnp.bfloat16)
    cols_second = make_patches(hidden.reshape(maps.shape))
    pre_second = jnp.dot(cols_second, w_second, preferred_element_type=jnp.float32)
    skip = maps.reshape(pre_second.shape).astype(jnp.float32)
    result = swish(skip + respond(pre_second, gains[1], biases[1], count)).astype(jnp.bfloat16)
    return (result.reshape(maps.shape), (cols_first, pre_first, cols_second, pre_second))

def block_backward(maps, cotangent, weights, gains, biases):
    count = maps.shape[0]
    w_first = weights[0].astype(jnp.bfloat16)
    w_second = weights[1].astype(jnp.bfloat16)
    saved = block_forward(maps, weights, gains, biases)[1]
    cols_first, pre_first, cols_second, pre_second = saved

    def second_part(values, skip, gain, bias):
        return swish(skip + respond(values, gain, bias, count))

    def first_part(values, gain, bias):
        return swish(respond(values, gain, bias, count))
    skip = maps.reshape(pre_second.shape).astype(jnp.float32)
    back_second = jax.vjp(second_part, pre_second, skip, gains[1], biases[1])[1]
    d_second, d_skip, dg_second, db_second = back_second(cotangent.reshape(pre_second.shape).astype(jnp.float32))
    q_second = d_second.astype(jnp.bfloat16)
    dw_second = jnp.dot(cols_second.T, q_second, preferred_element_type=jnp.float32)
    d_hidden = fold_patches(jnp.dot(q_second, w_second.T, preferred_element_type=jnp.float32), maps.shape)
    back_first = jax.vjp(first_part, pre_first, gains[0], biases[0])[1]
    d_first, dg_first, db_first = back_first(d_hidden.reshape(pre_first.shape))
    q_first = d_first.astype(jnp.bfloat16)
    dw_first = jnp.dot(cols_first.T, q_first, preferred_element_type=jnp.float32)
    d_input = fold_patches(jnp.dot(q_first, w_first.T, preferred_element_type=jnp.float32), maps.shape)
    d_maps = (d_skip.reshape(maps.shape) + d_input).astype(jnp.bfloat16)
    d_norm = jnp.stack([jnp.stack([dg_first, db_first]), jnp.stack([dg_second, db_second])])
    return (d_maps, jnp.stack([dw_first, dw_second]), d_norm)

def head_grads(final, labels, head_w, head_b, total):
    count = final.shape[0]
    width = final.shape[3]
    pixels = final.shape[1] * final.shape[2]
    pooled = lax.optimization_barrier(jnp.mean(final.reshape(count, pixels, width).astype(jnp.float32), axis=1))
    logits = jnp.dot(pooled, head_w, precision=lax.Precision.HIGHEST) + head_b
    top = lax.optimization_barrier(jnp.max(logits, axis=1, keepdims=True))
    expo = jnp.exp(logits - top)
    probs = expo / lax.optimization_barrier(jnp.sum(expo, axis=1, keepdims=True))
    onehot = (labels[:, None] == jnp.arange(head_w.shape[1])[None, :]).astype(jnp.float32)
    d_logits = (probs - onehot) / total
    d_head_w = jnp.dot(pooled.T, d_logits, precision=lax.Precision.HIGHEST)
    d_head_b = lax.optimization_barrier(jnp.sum(d_logits, axis=0))
    d_pooled = jnp.dot(d_logits, head_w.T, precision=lax.Precision.HIGHEST) / pixels
    spread = jnp.broadcast_to(d_pooled[:, None, :], (count, pixels, width))
    return (spread.astype(jnp.bfloat16).reshape(final.shape), d_head_w, d_head_b)

def group_grads(maps, labels, weights, gains, biases, head_w, head_b, total):
    saved = []
    for index in range(weights.shape[0]):
        saved.append(maps)
        maps = block_forward(maps, weights[index], gains[index], biases[index])[0]
    cotangent, d_head_w, d_head_b = head_grads(maps, labels, head_w, head_b, total)
    conv_terms = []
    norm_terms = []
    for index in reversed(range(weights.shape[0])):
        cotangent, d_conv, d_norm = block_backward(saved[index], cotangent, weights[index], gains[index], biases[index])
        conv_terms.insert(0, d_conv)
        norm_terms.insert(0, d_norm)
    return (jnp.stack(conv_terms), jnp.stack(norm_terms), d_head_w, d_head_b)

def accumulate(maps, labels, weights, gains, biases, head_w, head_b, total):
    width = weights.shape[3]
    initial = (jnp.zeros(weights.shape, jnp.float32), jnp.zeros((weights.shape[0], 2, 2, width), jnp.float32), jnp.zeros(head_w.shape, jnp.float32), jnp.zeros(head_b.shape, jnp.float32))

    def advance(carry, item):
        terms = group_grads(item[0], item[1], weights, gains, biases, head_w, head_b, total)
        return (tuple((left + right for left, right in zip(carry, terms))), None)
    return lax.scan(advance, initial, (maps, labels))[0]

def reference(images_in, labels, conv_weight, frn_gain, frn_bias, head_weight, head_bias):
    group_size = IMG_DEV // MICRO
    groups = IMAGES // group_size
    maps = images_in.reshape(groups, group_size, SIDE, SIDE, C)
    label_groups = labels.reshape(groups, group_size)
    conv_sum, norm_sum, head_w_sum, head_b_sum = accumulate(maps, label_groups, conv_weight, frn_gain, frn_bias, head_weight, head_bias, IMAGES)
    params = jnp.stack([frn_gain, frn_bias], axis=2)
    return (conv_sum + prior_precision * conv_weight, norm_sum + prior_precision * params, head_w_sum + prior_precision * head_weight, head_b_sum + prior_precision * head_bias)
```

```python
import functools

import jax
import jax.numpy as jnp
from jax import lax
from jax.experimental import pallas as pl
from jax.experimental.pallas import tpu as pltpu
from jax.sharding import PartitionSpec as P

F32 = jnp.float32
BF16 = jnp.bfloat16
MESH = pl.DeviceIdType.MESH
eps = 1e-06
prior_precision = 0.5
OFFSETS = (0, 1, 2, -1)


CHUNKS = ((5, 4), (3, 2), (1,), (0,))


def chunk_tiles(c):
    return 9 * len(CHUNKS[c]) + (3 if c == 0 else 1)


def kernel(total, dps, secs, img_hbm, labels, own_hbm, gain, bias, hw, hb, conv_out, small,
           xs, zs, dsw, rs, wf, wb, qs, qt, du2, du1, hw2, lab, wt, buf, in_a, tot, in_b,
           fin, img, own, load, w_send, w_recv, a_send, a_recv, b_send, b_recv, c_send, c_recv):
    dp, sec = lax.axis_index("dp"), lax.axis_index("section")
    per = [-(-chunk_tiles(c) // dps) for c in range(len(CHUNKS))]

    load_own = pltpu.make_async_copy(own_hbm, own, load.at[0])
    load_img = pltpu.make_async_copy(img_hbm, img, load.at[1])
    load_own.start()
    load_img.start()
    barrier = pltpu.get_barrier_semaphore()
    for d in range(1, secs):
        pl.semaphore_signal(barrier, inc=1, device_id=(dp, lax.rem(sec + d, secs)),
                            device_id_type=MESH)

    def greet(d, carry):
        pl.semaphore_signal(barrier, inc=1, device_id=(lax.rem(dp + d, dps), sec),
                            device_id_type=MESH)
        return carry

    lax.fori_loop(1, dps, greet, 0)
    load_own.wait()
    wt[sec] = own[...].astype(BF16)
    pl.semaphore_wait(barrier, secs - 1 + dps - 1)

    def send_w(b, d):
        mine = wt.at[sec, pl.ds(2 * b, 2)]
        return pltpu.make_async_remote_copy(
            src_ref=mine, dst_ref=mine, send_sem=w_send.at[b, d - 1],
            recv_sem=w_recv.at[b, d - 1], device_id=(dp, lax.rem(sec + d, secs)),
            device_id_type=MESH)

    def send_a(b, d):
        to = lax.rem(sec + d, secs)
        return pltpu.make_async_remote_copy(
            src_ref=buf.at[b, to, pl.ds(0, chunk_tiles(b))],
            dst_ref=in_a.at[b, d - 1, pl.ds(0, chunk_tiles(b))], send_sem=a_send.at[b, d - 1],
            recv_sem=a_recv.at[b, d - 1], device_id=(dp, to), device_id_type=MESH)

    def send_b(b, d):
        to = lax.rem(dp + d, dps)
        return pltpu.make_async_remote_copy(
            src_ref=tot.at[b, pl.ds(to * per[b], per[b])],
            dst_ref=in_b.at[b, d - 1, pl.ds(0, per[b])],
            send_sem=b_send.at[b, d - 1], recv_sem=b_recv.at[b, d - 1],
            device_id=(to, sec), device_id_type=MESH)

    def send_c(b, d):
        to = lax.rem(dp + d, dps)
        mine = fin.at[b, pl.ds(dp * per[b], per[b])]
        return pltpu.make_async_remote_copy(
            src_ref=mine, dst_ref=mine, send_sem=c_send.at[b, d - 1],
            recv_sem=c_recv.at[b, d - 1], device_id=(to, sec), device_id_type=MESH)

    def each_dp(act):
        def step(d, carry):
            act(d)
            return carry
        lax.fori_loop(1, dps, step, 0)

    def start_a(b):
        for d in range(1, secs):
            send_a(b, d).start()

    def start_b(b):
        for d in range(1, secs):
            send_a(b, d).wait_recv()
        tiles = chunk_tiles(b)
        all_terms = buf[b, sec, 0:tiles]
        for d in range(1, secs):
            all_terms = all_terms + in_a[b, d - 1, 0:tiles]
        tot[b, 0:tiles] = all_terms
        if tot.shape[1] > tiles:
            tot[b, tiles:] = jnp.zeros((tot.shape[1] - tiles, 8, 128), F32)
        each_dp(lambda d: send_b(b, d).start())

    def start_c(b):
        each_dp(lambda d: send_b(b, d).wait_recv())
        sums = lax.fori_loop(1, dps, lambda d, acc: acc + in_b[b, d - 1, 0:per[b]],
                             tot[b, pl.ds(dp * per[b], per[b])])
        fin[b, pl.ds(dp * per[b], per[b])] = sums
        each_dp(lambda d: send_c(b, d).start())

    def end_c(b):
        each_dp(lambda d: send_c(b, d).wait_recv())

    for b in range(3):
        for d in range(1, secs):
            send_w(b, d).start()
    lane = lax.broadcasted_iota(jnp.int32, (1, 128), 1)
    low = lane < 64

    def both(v):
        return v + pltpu.roll(v, 64, 1)

    def twice(v):
        return jnp.concatenate([v, v], axis=1)

    for ref in (qs, qt):
        ref[0] = jnp.zeros(ref.shape[1:], BF16)
        ref[9] = jnp.zeros(ref.shape[1:], BF16)
    for k in range(6):
        xs[k, 0] = jnp.zeros((256, 256), BF16)
        xs[k, 9] = jnp.zeros((256, 256), BF16)

    def put(ref, y, v):
        edge = jnp.zeros((1, 64, 128), F32)
        after = jnp.concatenate([v[1:], edge], axis=0)
        before = jnp.concatenate([edge, v[:3]], axis=0)
        beside = jnp.where(low[None], after, before)
        ref[y + 1, :, 0:128] = v.reshape(256, 128).astype(BF16)
        ref[y + 1, :, 128:256] = beside.reshape(256, 128).astype(BF16)

    def conv(src, w, body, init):
        def run(*accs):
            for m in range(2):
                for kt in range(2):
                    at = (2 * m + kt) * 256
                    pltpu.matmul_push_rhs(w[at:at + 256, :], kt, m)
            for kt in range(2):
                for y2 in range(4):
                    for m in range(2):
                        pltpu.matmul_acc_lhs(accs[4 * m + y2], src[2 * y2 + 2 * m + kt],
                                             load_staged_rhs=kt if y2 == 0 else None)
            carry = init
            for y2 in range(4):
                out = pltpu.matmul_pop(accs[y2]) + pltpu.matmul_pop(accs[4 + y2])
                for yo in range(2):
                    carry = body(2 * y2 + yo, out[:, yo * 128:yo * 128 + 128], carry)
            return carry

        return pl.run_scoped(run, *[pltpu.ACC(m)((256, 256), F32) for m in range(2) for _ in range(4)])

    def split(v):
        top = v.astype(BF16)
        return [top, (v - top.astype(F32)).astype(BF16)]

    def dot_f32(a, b):
        def run(acc):
            half = jnp.concatenate(split(b), axis=1)
            pltpu.matmul_push_rhs(jnp.concatenate([half, half], axis=0), 0, 0)
            pltpu.matmul_acc_lhs(acc, jnp.concatenate(split(a), axis=1), load_staged_rhs=0)
            out = pltpu.matmul_pop(acc)
            return out[:, 0:128] + out[:, 128:256]

        return pl.run_scoped(run, pltpu.ACC(0)((a.shape[0], 256), F32))

    zero_sum = jnp.zeros((64, 128), F32)

    def over_pairs(v):
        return jnp.sum(v.reshape(4, 64, 128), axis=0)

    load_img.wait()
    for y in range(8):
        slab = jnp.stack([img[:, (y * 4 + j) * 128:(y * 4 + j + 1) * 128]
                          for j in range(4)], axis=0).astype(F32)
        put(xs.at[0], y, slab)

    def spread(b):
        for d in range(1, secs):
            send_w(b, d).wait_recv()
        flat = jnp.concatenate(
            [wt[q, 2 * b + j] for j in range(2) for q in range(secs)], axis=0).astype(F32)
        zero = jnp.zeros((64, 128), BF16)
        cols = jnp.concatenate([flat, jnp.zeros((128, 64), F32)], axis=1).T
        plain = [cols[t * 64:(t + 1) * 64] for t in range(9)]
        turned = [pltpu.roll(v, 64, 1) for v in plain]
        none = jnp.zeros((64, 128), F32)
        for j in range(2):
            first, second = (plain, turned) if j == 0 else (turned, plain)
            for a in range(3):
                for s, xi in enumerate(OFFSETS):
                    left = first[a * 3 + xi + 1] if 0 <= xi + 1 <= 2 else none
                    right = second[a * 3 + xi] if 0 <= xi <= 2 else none
                    tile = jnp.where(low, left, right).astype(BF16)
                    for yo in range(2):
                        row = (a + yo) * 256 + s * 64
                        wf[2 * b + j, row:row + 64, yo * 128:yo * 128 + 128] = tile
        wide = jnp.concatenate(
            [jnp.zeros((128, 64), F32), flat, jnp.zeros((128, 128), F32)], axis=1)
        for a in range(3):
            for s, xi in enumerate(OFFSETS):
                at = ((2 - a) * 3 + 2 - xi) * 64
                tile = wide[:, at:at + 128]
                if xi == -1:
                    tile = jnp.where(low, tile, 0.0)
                if xi == 2:
                    tile = jnp.where(low, 0.0, tile)
                tile = tile.astype(BF16)
                for j in range(2):
                    for yo in range(2):
                        row = (a + yo) * 256 + s * 64
                        wb[2 * b + j, row:row + 64, yo * 128:yo * 128 + 128] = (
                            tile[j * 64:j * 64 + 64])
        for j in range(2):
            for ref in (wf, wb):
                for s in range(4):
                    ref[2 * b + j, 768 + s * 64:832 + s * 64, 0:128] = zero
                    ref[2 * b + j, s * 64:s * 64 + 64, 128:256] = zero

    pooled = zero_sum
    for k in range(6):
        b, j = k // 2, k % 2
        if j == 0:
            spread(b)

        def keep(y, out, energy):
            zs[k, y] = out
            return energy + over_pairs(out * out)

        energy = conv(xs.at[k], wf.at[k], keep, zero_sum)
        r = lax.rsqrt(both(energy) * (1.0 / 64) + eps)
        rs[k] = r
        scale = r * twice(gain[b, j:j + 1, :])
        shift = twice(bias[b, j:j + 1, :])

        def activate(y, carry):
            u = zs[k, y].reshape(4, 64, 128) * scale[None] + shift[None]
            if j == 1:
                u = u + xs[k - 1, y + 1, :, 0:128].astype(F32).reshape(4, 64, 128)
            sig = 0.5 * jnp.tanh(0.5 * u) + 0.5
            out = u * sig
            dsw[k, y] = (sig + out * (1.0 - sig)).reshape(256, 128)
            if k < 5:
                put(xs.at[k + 1], y, out)
                return carry
            return carry + jnp.sum(out.astype(BF16).astype(F32), axis=0)

        pooled = lax.fori_loop(0, 8, activate, pooled)

    pooled = both(pooled) * (1.0 / 64)
    hw2[...] = jnp.zeros((128, 128), F32)
    hw2[0:hw.shape[0], :] = twice(hw[...])
    lab[...] = jnp.zeros((8, 128), jnp.int32)
    lab[0:1, 0:64] = labels[...]
    classes = hw.shape[0]
    hbias = jnp.concatenate([hb[...], jnp.zeros((1, 128 - classes), F32)], axis=1)
    logits = dot_f32(jnp.where(low, pooled, 0.0), hw2[...].T) + hbias
    live = lane < classes
    logits = jnp.where(live, logits, -1e30)
    top = jnp.max(logits, axis=1, keepdims=True)
    expo = jnp.where(live, jnp.exp(logits - top), 0.0)
    probs = expo / jnp.sum(expo, axis=1, keepdims=True)
    onehot = jnp.where(
        lax.broadcasted_iota(jnp.int32, (128, 128), 0) == lab[0:1, :], 1.0, 0.0).T
    dl = (probs - onehot[0:64]) * (1.0 / total)
    dlt = jnp.concatenate([dl, jnp.zeros((64, 128), F32)], axis=0).T
    tall = jnp.concatenate([pooled, jnp.zeros((64, 128), F32)], axis=0)
    d_head = dot_f32(dlt[0:16], tall)
    row = lax.broadcasted_iota(jnp.int32, (8, 128), 0)
    extra = jnp.where(row == 4, jnp.sum(dl, axis=0, keepdims=True), 0.0)
    for q in range(secs):
        buf[0, q, 19] = d_head[0:8]
        buf[0, q, 20] = d_head[8:16]
    spread_g = dot_f32(dl, hw2[...]) * (1.0 / 64)
    spread_g = spread_g.astype(BF16).astype(F32)

    def tally(k, y, d, sums):
        return (sums[0] + over_pairs(d * zs[k, y]), sums[1] + over_pairs(d))

    def begin(y, sums):
        d = (dsw[5, y].reshape(4, 64, 128) * spread_g[None]).reshape(256, 128)
        du2[y] = d
        return tally(5, y, d, sums)

    sums = lax.fori_loop(0, 8, begin, (zero_sum, zero_sum))
    for k in range(5, -1, -1):
        b, j = k // 2, k % 2
        source = du2 if j == 1 else du1
        c = [k in ks for ks in CHUNKS].index(True)
        at_tile = CHUNKS[c].index(k)
        ends = k == CHUNKS[c][-1]
        r = rs[k]
        dg = both(sums[0]) * r
        db = both(sums[1])
        extra = jnp.where(row == 2 * at_tile, jnp.sum(dg, axis=0, keepdims=True), extra)
        extra = jnp.where(row == 2 * at_tile + 1, jnp.sum(db, axis=0, keepdims=True), extra)
        if ends:
            for q in range(secs):
                buf[c, q, 9 * len(CHUNKS[c])] = extra
            extra = jnp.zeros((8, 128), F32)
        c1 = r * twice(gain[b, j:j + 1, :])
        c2 = c1 * dg * r * (1.0 / 64)

        def settle(y, carry):
            d = (source[y].reshape(4, 64, 128) * c1[None]
                 - zs[k, y].reshape(4, 64, 128) * c2[None])
            if k > 0:
                put(qs, y, d)
            qt[y + 1] = d.reshape(256, 128).T.astype(BF16)
            return carry

        lax.fori_loop(0, 8, settle, 0)

        def weight_terms(*accs):
            for step in range(4):
                for m in range(2):
                    y = 2 * step + m
                    pltpu.matmul_push_rhs(xs[k, y + 1], step % 2, m)
                    for a in range(3):
                        pltpu.matmul_acc_lhs(accs[3 * m + a], qt[y - a + 2],
                                             load_staged_rhs=step % 2 if a == 0 else None)
            return jnp.concatenate(
                [pltpu.matmul_pop(accs[a]) + pltpu.matmul_pop(accs[3 + a]) for a in range(3)], axis=0)

        terms = pl.run_scoped(
            weight_terms, *[pltpu.ACC(m)((128, 256), F32) for m in range(2) for _ in range(3)])
        for a in range(3):
            zero_side = pltpu.roll(terms[a * 128:a * 128 + 64], 64, 1)
            both_sides = zero_side + terms[a * 128 + 64:a * 128 + 128]
            for e in range(3):
                at = e // 2 * 128
                here = both_sides[:, at:at + 128]
                there = pltpu.roll(here, 64, 1)
                first, second = (here, there) if e % 2 == 0 else (there, here)
                for q in range(secs):
                    buf[c, q, at_tile * 9 + a * 3 + e] = jnp.where(
                        low, first[q * 16:q * 16 + 8], second[q * 16 + 8:q * 16 + 16])

        if ends:
            start_a(c)
        if k == 3:
            start_b(0)
        if k == 2:
            start_c(0)

        if j == 1:
            def to_first(y, out, sums):
                d = out * dsw[k - 1, y]
                du1[y] = d
                return tally(k - 1, y, d, sums)

            sums = conv(qs, wb.at[k], to_first, (zero_sum, zero_sum))
            if k == 1:
                start_b(1)
        elif k > 0:
            def to_second(y, out, sums):
                g = (du2[y] + out).astype(BF16).astype(F32)
                d = g * dsw[k - 1, y]
                du2[y] = d
                return tally(k - 1, y, d, sums)

            sums = conv(qs, wb.at[k], to_second, (zero_sum, zero_sum))

    start_c(1)
    start_b(2)
    start_b(3)
    start_c(2)
    start_c(3)
    for c, ks in enumerate(CHUNKS):
        end_c(c)
        for at_tile, k in enumerate(ks):
            rows = [fin[c, at_tile * 9 + t] for t in range(9)]
            conv_out[k, 0:8] = jnp.concatenate([v[:, 0:64] for v in rows], axis=1)
            conv_out[k, 8:16] = jnp.concatenate([v[:, 64:128] for v in rows], axis=1)
            small[2 * k:2 * k + 2] = fin[c, 9 * len(ks)][2 * at_tile:2 * at_tile + 2]
        if c == 0:
            small[12:13] = fin[c, 18][4:5]
            small[16:24] = fin[c, 19]
            small[24:32] = fin[c, 20]
    for b in range(3):
        for d in range(1, secs):
            send_w(b, d).wait_send()
    for c in range(len(CHUNKS)):
        for d in range(1, secs):
            send_a(c, d).wait_send()
        each_dp(lambda d: send_b(c, d).wait_send())
        each_dp(lambda d: send_c(c, d).wait_send())


def all_grads(total, dps, secs, images_in, labels, own, gain, bias, hw, hb):
    vmem = pl.BlockSpec(memory_space=pltpu.VMEM)
    chunks = len(CHUNKS)
    tiles = max(chunk_tiles(c) for c in range(chunks))
    per = -(-tiles // dps)
    hbm = pl.BlockSpec(memory_space=pltpu.HBM)
    dma = pltpu.SemaphoreType.DMA
    return pl.pallas_call(
        functools.partial(kernel, total, dps, secs),
        out_shape=(jax.ShapeDtypeStruct(own.shape, F32),
                   jax.ShapeDtypeStruct((32, 128), F32)),
        in_specs=[hbm, vmem, hbm, vmem, vmem, vmem, vmem],
        out_specs=(vmem, vmem),
        scratch_shapes=[
            pltpu.VMEM((6, 10, 256, 256), BF16),
            pltpu.VMEM((6, 8, 256, 128), F32),
            pltpu.VMEM((6, 8, 256, 128), F32),
            pltpu.VMEM((6, 64, 128), F32),
            pltpu.VMEM((6, 1024, 256), BF16),
            pltpu.VMEM((6, 1024, 256), BF16),
            pltpu.VMEM((10, 256, 256), BF16),
            pltpu.VMEM((10, 128, 256), BF16),
            pltpu.VMEM((8, 256, 128), F32),
            pltpu.VMEM((8, 256, 128), F32),
            pltpu.VMEM((128, 128), F32),
            pltpu.VMEM((8, 128), jnp.int32),
            pltpu.VMEM((secs,) + own.shape, BF16),
            pltpu.VMEM((chunks, secs, tiles, 8, 128), F32),
            pltpu.VMEM((chunks, secs - 1, tiles, 8, 128), F32),
            pltpu.VMEM((chunks, per * dps, 8, 128), F32),
            pltpu.VMEM((chunks, dps - 1, per, 8, 128), F32),
            pltpu.VMEM((chunks, per * dps, 8, 128), F32),
            pltpu.VMEM(images_in.shape, BF16),
            pltpu.VMEM(own.shape, F32),
            dma((2,)),
            dma((3, secs - 1)), dma((3, secs - 1)),
            dma((chunks, secs - 1)), dma((chunks, secs - 1)),
            dma((chunks, dps - 1)), dma((chunks, dps - 1)),
            dma((chunks, dps - 1)), dma((chunks, dps - 1)),
        ],
        compiler_params=pltpu.CompilerParams(
            vmem_limit_bytes=63 * 1024 * 1024 + 768 * 1024, collective_id=0, has_side_effects=True),
    )(images_in, labels, own, gain, bias, hw, hb)


def per_device(images_in, labels, conv_weight, frn_gain, frn_bias, head_weight, head_bias):
    images = images_in.shape[0]
    dps, secs = lax.axis_size("dp"), lax.axis_size("section")
    blocks, convs, depth, share = conv_weight.shape
    own = jnp.swapaxes(conv_weight, 2, 3).reshape(blocks * convs, share, depth)
    owned, small = all_grads(images * dps * secs, dps, secs, images_in,
                             labels.reshape(1, images), own, frn_gain,
                             frn_bias, head_weight.T, head_bias.reshape(1, -1))
    classes = head_bias.shape[0]
    params = jnp.stack([frn_gain, frn_bias], axis=2)
    return (
        jnp.swapaxes(owned.reshape(blocks, convs, share, depth), 2, 3)
        + prior_precision * conv_weight,
        small[0:12, 0:64].reshape(params.shape)
        + prior_precision * params,
        small[16:16 + classes, 0:64].T + prior_precision * head_weight,
        small[12, 0:classes] + prior_precision * head_bias,
    )


def solution(mesh):
    return jax.shard_map(
        per_device,
        mesh=mesh,
        in_specs=(
            P(("dp", "section"), None),
            P(("dp", "section")),
            P(None, None, None, "section"),
            P(),
            P(),
            P(),
            P(),
        ),
        out_specs=(P(None, None, None, "section"), P(), P(), P()),
        check_vma=False,
    )
```

```python
import functools

import jax
import jax.numpy as jnp
from jax import lax
from jax.experimental import pallas as pl
from jax.experimental.pallas import tpu as pltpu
from jax.sharding import PartitionSpec as P

F32 = jnp.float32
BF16 = jnp.bfloat16
MESH = pl.DeviceIdType.MESH
eps = 1e-06
prior_precision = 0.5
OFFSETS = (0, 1, 2, -1)


TILES = 5
DIRECT = (1, 0)
AFTER = {3: (("b", 5),), 2: (("b", 4),), 1: (("b", 3),)}
TAIL = (("b", 2), ("c", 5), ("c", 4), ("b", 1), ("c", 3), ("b", 0), ("c", 2),
        ("f", 5), ("f", 4), ("f", 3), ("f", 2), ("f", 1), ("f", 0))


def owner(k, m, dps):
    return (m * dps // TILES + 3 * k) % dps


def kernel(total, dps, secs, img_hbm, labels, own_hbm, gain, bias, hw, hb,
           conv_out, norm_out, hw_out, hb_out,
           xs, zs, dsw, rs, wf, wb, qs, qt, du2, du1, hw2, lab, wt, buf, in_a, tot, in_b,
           fin, img, own, load, w_send, w_recv, a_send, a_recv, b_send, b_recv, c_send, c_recv):
    dp, sec = lax.axis_index("dp"), lax.axis_index("section")
    lane = lax.broadcasted_iota(jnp.int32, (1, 128), 1)
    low = lane < 64
    classes = hw.shape[0]

    load_own = pltpu.make_async_copy(own_hbm, own, load.at[0])
    load_img = pltpu.make_async_copy(img_hbm, img, load.at[1])
    load_own.start()
    load_img.start()
    barrier = pltpu.get_barrier_semaphore()
    for d in range(1, secs):
        pl.semaphore_signal(barrier, inc=1, device_id=(dp, lax.rem(sec + d, secs)),
                            device_id_type=MESH)

    def greet(d, carry):
        pl.semaphore_signal(barrier, inc=1, device_id=(lax.rem(dp + d, dps), sec),
                            device_id_type=MESH)
        return carry

    lax.fori_loop(1, dps, greet, 0)
    load_own.wait()
    wt[sec] = own[...].astype(BF16)
    pl.semaphore_wait(barrier, secs - 1 + dps - 1)

    def send_w(b, d):
        mine = wt.at[sec, pl.ds(2 * b, 2)]
        return pltpu.make_async_remote_copy(
            src_ref=mine, dst_ref=mine, send_sem=w_send.at[b, d - 1],
            recv_sem=w_recv.at[b, d - 1], device_id=(dp, lax.rem(sec + d, secs)),
            device_id_type=MESH)

    def send_a(k, d):
        to = lax.rem(sec + d, secs)
        return pltpu.make_async_remote_copy(
            src_ref=buf.at[k, to], dst_ref=in_a.at[k, sec], send_sem=a_send.at[k, d - 1],
            recv_sem=a_recv.at[k, d - 1], device_id=(dp, to), device_id_type=MESH)

    def send_tile(k, m):
        to = owner(k, m, dps)
        return pltpu.make_async_remote_copy(
            src_ref=tot.at[k, m], dst_ref=in_b.at[k, dp, m], send_sem=b_send.at[k, m],
            recv_sem=b_recv.at[k, lax.rem(to - dp + dps - 1, dps)],
            device_id=(to, sec), device_id_type=MESH)

    def wait_tile(k, m, d):
        pltpu.make_async_remote_copy(
            src_ref=tot.at[k, m], dst_ref=in_b.at[k, lax.rem(dp - d + dps, dps), m],
            send_sem=b_send.at[k, m], recv_sem=b_recv.at[k, d - 1],
            device_id=(lax.rem(dp + d, dps), sec), device_id_type=MESH).wait_recv()

    def send_all(k, d):
        to = lax.rem(dp + d, dps)
        return pltpu.make_async_remote_copy(
            src_ref=tot.at[k], dst_ref=in_b.at[k, dp], send_sem=b_send.at[k, d - 1],
            recv_sem=b_recv.at[k, d - 1], device_id=(to, sec), device_id_type=MESH)

    def send_c(k, m, d):
        return pltpu.make_async_remote_copy(
            src_ref=fin.at[k, m], dst_ref=fin.at[k, m], send_sem=c_send.at[k, d - 1],
            recv_sem=c_recv.at[k, m], device_id=(lax.rem(dp + d, dps), sec),
            device_id_type=MESH)

    def each_dp(act):
        def step(d, carry):
            act(d)
            return carry
        lax.fori_loop(1, dps, step, 0)

    def resplit(v):
        whole = v[0:8] + v[8:16]
        top = whole.astype(BF16).astype(F32)
        return jnp.where(low, v, jnp.concatenate([top, whole - top], axis=0))

    def start_a(k):
        for d in range(1, secs):
            send_a(k, d).start()
        in_a[k, sec] = buf[k, sec]

    def start_b(k):
        for d in range(1, secs):
            send_a(k, d).wait_recv()
        for m in range(TILES):
            v = in_a[k, 0, m].astype(F32)
            for q in range(1, secs):
                v = v + in_a[k, q, m].astype(F32)
            tot[k, m] = (resplit(v) if m == TILES - 1 else v).astype(BF16)
        if k in DIRECT:
            each_dp(lambda d: send_all(k, d).start())
            in_b[k, dp] = tot[k]
            return
        for m in range(TILES):
            @pl.when(dp != owner(k, m, dps))
            def _():
                send_tile(k, m).start()

            @pl.when(dp == owner(k, m, dps))
            def _():
                in_b[k, dp, m] = tot[k, m]

    def sum_b(k, m):
        v = lax.fori_loop(1, dps, lambda p, acc: acc + in_b[k, p, m].astype(F32),
                          in_b[k, 0, m].astype(F32))
        fin[k, m] = (resplit(v) if m == TILES - 1 else v).astype(BF16)

    def start_c(k):
        for m in range(TILES):
            @pl.when(dp == owner(k, m, dps))
            def _():
                each_dp(lambda d: wait_tile(k, m, d))
                sum_b(k, m)
                each_dp(lambda d: send_c(k, m, d).start())

    def finish(k):
        if k in DIRECT:
            each_dp(lambda d: pltpu.make_async_remote_copy(
                src_ref=tot.at[k], dst_ref=in_b.at[k, lax.rem(dp - d + dps, dps)],
                send_sem=b_send.at[k, d - 1], recv_sem=b_recv.at[k, d - 1],
                device_id=(lax.rem(dp + d, dps), sec), device_id_type=MESH).wait_recv())
            for m in range(TILES):
                sum_b(k, m)
        else:
            for m in range(TILES):
                @pl.when(dp != owner(k, m, dps))
                def _():
                    send_c(k, m, 1).wait_recv()
        rows = [fin[k, m].astype(F32) for m in range(TILES)]
        side = pltpu.roll(rows[-1][0:8] + rows[-1][8:16], 64, 1)[:, 0:64]
        conv_out[k] = (jnp.concatenate(rows[:-1] + [rows[-1][:, 0:64]], axis=1)
                       + prior_precision * own[k])
        b, j = k // 2, k % 2
        norm_out[b, j, 0:1] = side[0:1] + prior_precision * gain[b, j:j + 1, :]
        norm_out[b, j, 1:2] = side[1:2] + prior_precision * bias[b, j:j + 1, :]
        if k == 5:
            hw_out[0:6] = side[2:8] + prior_precision * hw[0:6]
        if k == 4:
            hw_out[6:classes] = side[2:classes - 4] + prior_precision * hw[6:classes]
            hb_out[...] = side[6:7, 0:classes] + prior_precision * hb[...]

    for b in range(3):
        for d in range(1, secs):
            send_w(b, d).start()

    def both(v):
        return v + pltpu.roll(v, 64, 1)

    def twice(v):
        return jnp.concatenate([v, v], axis=1)

    for ref in (qs, qt):
        ref[0] = jnp.zeros(ref.shape[1:], BF16)
        ref[9] = jnp.zeros(ref.shape[1:], BF16)
    for k in range(6):
        xs[k, 0] = jnp.zeros((256, 256), BF16)
        xs[k, 9] = jnp.zeros((256, 256), BF16)

    def put(ref, y, v):
        edge = jnp.zeros((1, 64, 128), F32)
        after = jnp.concatenate([v[1:], edge], axis=0)
        before = jnp.concatenate([edge, v[:3]], axis=0)
        beside = jnp.where(low[None], after, before)
        ref[y + 1, :, 0:128] = v.reshape(256, 128).astype(BF16)
        ref[y + 1, :, 128:256] = beside.reshape(256, 128).astype(BF16)

    def conv(src, w, body, init):
        def run(*accs):
            for m in range(2):
                for kt in range(2):
                    at = (2 * m + kt) * 256
                    pltpu.matmul_push_rhs(w[at:at + 256, :], kt, m)
            for kt in range(2):
                for y2 in range(4):
                    for m in range(2):
                        pltpu.matmul_acc_lhs(accs[4 * m + y2], src[2 * y2 + 2 * m + kt],
                                             load_staged_rhs=kt if y2 == 0 else None)
            carry = init
            for y2 in range(4):
                out = pltpu.matmul_pop(accs[y2]) + pltpu.matmul_pop(accs[4 + y2])
                for yo in range(2):
                    carry = body(2 * y2 + yo, out[:, yo * 128:yo * 128 + 128], carry)
            return carry

        return pl.run_scoped(run, *[pltpu.ACC(m)((256, 256), F32) for m in range(2) for _ in range(4)])

    def split(v):
        top = v.astype(BF16)
        return [top, (v - top.astype(F32)).astype(BF16)]

    def dot_f32(a, b):
        def run(acc):
            half = jnp.concatenate(split(b), axis=1)
            pltpu.matmul_push_rhs(jnp.concatenate([half, half], axis=0), 0, 0)
            pltpu.matmul_acc_lhs(acc, jnp.concatenate(split(a), axis=1), load_staged_rhs=0)
            out = pltpu.matmul_pop(acc)
            return out[:, 0:128] + out[:, 128:256]

        return pl.run_scoped(run, pltpu.ACC(0)((a.shape[0], 256), F32))

    zero_sum = jnp.zeros((64, 128), F32)

    def over_pairs(v):
        return jnp.sum(v.reshape(4, 64, 128), axis=0)

    load_img.wait()
    for y in range(8):
        slab = jnp.stack([img[:, (y * 4 + j) * 128:(y * 4 + j + 1) * 128]
                          for j in range(4)], axis=0).astype(F32)
        put(xs.at[0], y, slab)

    def spread(b):
        for d in range(1, secs):
            send_w(b, d).wait_recv()
        flat = jnp.concatenate(
            [wt[q, 2 * b + j] for j in range(2) for q in range(secs)], axis=0).astype(F32)
        zero = jnp.zeros((64, 128), BF16)
        cols = jnp.concatenate([flat, jnp.zeros((128, 64), F32)], axis=1).T
        plain = [cols[t * 64:(t + 1) * 64] for t in range(9)]
        turned = [pltpu.roll(v, 64, 1) for v in plain]
        none = jnp.zeros((64, 128), F32)
        for j in range(2):
            first, second = (plain, turned) if j == 0 else (turned, plain)
            for a in range(3):
                for s, xi in enumerate(OFFSETS):
                    left = first[a * 3 + xi + 1] if 0 <= xi + 1 <= 2 else none
                    right = second[a * 3 + xi] if 0 <= xi <= 2 else none
                    tile = jnp.where(low, left, right).astype(BF16)
                    for yo in range(2):
                        row = (a + yo) * 256 + s * 64
                        wf[2 * b + j, row:row + 64, yo * 128:yo * 128 + 128] = tile
        wide = jnp.concatenate(
            [jnp.zeros((128, 64), F32), flat, jnp.zeros((128, 128), F32)], axis=1)
        for a in range(3):
            for s, xi in enumerate(OFFSETS):
                at = ((2 - a) * 3 + 2 - xi) * 64
                tile = wide[:, at:at + 128]
                if xi == -1:
                    tile = jnp.where(low, tile, 0.0)
                if xi == 2:
                    tile = jnp.where(low, 0.0, tile)
                tile = tile.astype(BF16)
                for j in range(2):
                    for yo in range(2):
                        row = (a + yo) * 256 + s * 64
                        wb[2 * b + j, row:row + 64, yo * 128:yo * 128 + 128] = (
                            tile[j * 64:j * 64 + 64])
        for j in range(2):
            for ref in (wf, wb):
                for s in range(4):
                    ref[2 * b + j, 768 + s * 64:832 + s * 64, 0:128] = zero
                    ref[2 * b + j, s * 64:s * 64 + 64, 128:256] = zero

    pooled = zero_sum
    for k in range(6):
        b, j = k // 2, k % 2
        if j == 0:
            spread(b)

        def keep(y, out, energy):
            zs[k, y] = out
            return energy + over_pairs(out * out)

        energy = conv(xs.at[k], wf.at[k], keep, zero_sum)
        r = lax.rsqrt(both(energy) * (1.0 / 64) + eps)
        rs[k] = r
        scale = r * twice(gain[b, j:j + 1, :])
        shift = twice(bias[b, j:j + 1, :])

        def activate(y, carry):
            u = zs[k, y].reshape(4, 64, 128) * scale[None] + shift[None]
            if j == 1:
                u = u + xs[k - 1, y + 1, :, 0:128].astype(F32).reshape(4, 64, 128)
            sig = 0.5 * jnp.tanh(0.5 * u) + 0.5
            out = u * sig
            dsw[k, y] = (sig + out * (1.0 - sig)).reshape(256, 128)
            if k < 5:
                put(xs.at[k + 1], y, out)
                return carry
            return carry + jnp.sum(out.astype(BF16).astype(F32), axis=0)

        pooled = lax.fori_loop(0, 8, activate, pooled)

    pooled = both(pooled) * (1.0 / 64)
    hw2[...] = jnp.zeros((128, 128), F32)
    hw2[0:hw.shape[0], :] = twice(hw[...])
    lab[...] = jnp.zeros((8, 128), jnp.int32)
    lab[0:1, 0:64] = labels[...]
    hbias = jnp.concatenate([hb[...], jnp.zeros((1, 128 - classes), F32)], axis=1)
    logits = dot_f32(jnp.where(low, pooled, 0.0), hw2[...].T) + hbias
    live = lane < classes
    logits = jnp.where(live, logits, -1e30)
    top = jnp.max(logits, axis=1, keepdims=True)
    expo = jnp.where(live, jnp.exp(logits - top), 0.0)
    probs = expo / jnp.sum(expo, axis=1, keepdims=True)
    onehot = jnp.where(
        lax.broadcasted_iota(jnp.int32, (128, 128), 0) == lab[0:1, :], 1.0, 0.0).T
    dl = (probs - onehot[0:64]) * (1.0 / total)
    dlt = jnp.concatenate([dl, jnp.zeros((64, 128), F32)], axis=0).T
    tall = jnp.concatenate([pooled, jnp.zeros((64, 128), F32)], axis=0)
    d_head = dot_f32(dlt[0:16], tall)
    row = lax.broadcasted_iota(jnp.int32, (8, 128), 0)
    d_bias = pltpu.roll(jnp.sum(dl, axis=0, keepdims=True), 64, 1)
    head_rows = {
        5: jnp.where(row >= 2, pltpu.roll(d_head[0:8], 2, 0), 0.0),
        4: jnp.where(row == 6, d_bias,
                     jnp.where(row >= 4, pltpu.roll(d_head[8:16], 4, 0),
                               pltpu.roll(d_head[0:8], 4, 0))),
    }
    spread_g = dot_f32(dl, hw2[...]) * (1.0 / 64)
    spread_g = spread_g.astype(BF16).astype(F32)

    def advance(k):
        for act, other in AFTER.get(k, ()):
            {"b": start_b, "c": start_c}[act](other)

    def tally(k, y, d, sums):
        return (sums[0] + over_pairs(d * zs[k, y]), sums[1] + over_pairs(d))

    def begin(y, sums):
        d = (dsw[5, y].reshape(4, 64, 128) * spread_g[None]).reshape(256, 128)
        du2[y] = d
        return tally(5, y, d, sums)

    sums = lax.fori_loop(0, 8, begin, (zero_sum, zero_sum))
    for k in range(5, -1, -1):
        b, j = k // 2, k % 2
        source = du2 if j == 1 else du1
        r = rs[k]
        dg = both(sums[0]) * r
        db = both(sums[1])
        extra = jnp.where(row == 0, jnp.sum(dg, axis=0, keepdims=True),
                          jnp.where(row == 1, jnp.sum(db, axis=0, keepdims=True),
                                    head_rows.get(k, 0.0)))
        top = extra.astype(BF16).astype(F32)
        side = jnp.concatenate([top, extra - top] * secs, axis=0)
        c1 = r * twice(gain[b, j:j + 1, :])
        c2 = c1 * dg * r * (1.0 / 64)

        def settle(y, carry):
            d = (source[y].reshape(4, 64, 128) * c1[None]
                 - zs[k, y].reshape(4, 64, 128) * c2[None])
            if k > 0:
                put(qs, y, d)
            qt[y + 1] = d.reshape(256, 128).T.astype(BF16)
            return carry

        lax.fori_loop(0, 8, settle, 0)

        def weight_terms(*accs):
            for step in range(4):
                for m in range(2):
                    y = 2 * step + m
                    pltpu.matmul_push_rhs(xs[k, y + 1], step % 2, m)
                    for a in range(3):
                        pltpu.matmul_acc_lhs(accs[3 * m + a], qt[y - a + 2],
                                             load_staged_rhs=step % 2 if a == 0 else None)
            return jnp.concatenate(
                [pltpu.matmul_pop(accs[a]) + pltpu.matmul_pop(accs[3 + a]) for a in range(3)], axis=0)

        terms = pl.run_scoped(
            weight_terms, *[pltpu.ACC(m)((128, 256), F32) for m in range(2) for _ in range(3)])
        def rolled(a):
            return (pltpu.roll(terms[a * 128:a * 128 + 64], 64, 1)
                    + terms[a * 128 + 64:a * 128 + 128])

        first, last = rolled(0), rolled(2)
        swapped = jnp.concatenate([terms[128:192, 128:256], terms[128:192, 0:128]], axis=1)
        middle = swapped + pltpu.roll(terms[192:256], 64, 1)
        tiles = [first[:, 0:128], jnp.where(low, first[:, 128:256], middle[:, 0:128]),
                 middle[:, 128:256], last[:, 0:128], jnp.where(low, last[:, 128:256], side)]
        for m in range(TILES):
            v = tiles[m].astype(BF16)
            for q in range(secs):
                buf[k, q, m] = v[q * 16:q * 16 + 16]
        start_a(k)

        if j == 1:
            def to_first(y, out, sums):
                d = out * dsw[k - 1, y]
                du1[y] = d
                return tally(k - 1, y, d, sums)

            sums = conv(qs, wb.at[k], to_first, (zero_sum, zero_sum))
            advance(k)
        elif k > 0:
            def to_second(y, out, sums):
                g = (du2[y] + out).astype(BF16).astype(F32)
                d = g * dsw[k - 1, y]
                du2[y] = d
                return tally(k - 1, y, d, sums)

            sums = conv(qs, wb.at[k], to_second, (zero_sum, zero_sum))
            advance(k)

    for act, k in TAIL:
        {"b": start_b, "c": start_c, "f": finish}[act](k)
    for b in range(3):
        for d in range(1, secs):
            send_w(b, d).wait_send()
    for k in range(6):
        for d in range(1, secs):
            send_a(k, d).wait_send()
        if k in DIRECT:
            each_dp(lambda d: send_all(k, d).wait_send())
            continue
        for m in range(TILES):
            @pl.when(dp != owner(k, m, dps))
            def _():
                send_tile(k, m).wait_send()

            @pl.when(dp == owner(k, m, dps))
            def _():
                each_dp(lambda d: send_c(k, m, d).wait_send())


def all_grads(total, dps, secs, images_in, labels, own, gain, bias, hw, hb):
    vmem = pl.BlockSpec(memory_space=pltpu.VMEM)
    hbm = pl.BlockSpec(memory_space=pltpu.HBM)
    dma = pltpu.SemaphoreType.DMA
    return pl.pallas_call(
        functools.partial(kernel, total, dps, secs),
        out_shape=(jax.ShapeDtypeStruct(own.shape, F32),
                   jax.ShapeDtypeStruct(gain.shape[:2] + (2,) + gain.shape[2:], F32),
                   jax.ShapeDtypeStruct(hw.shape, F32),
                   jax.ShapeDtypeStruct(hb.shape, F32)),
        in_specs=[hbm, vmem, hbm, vmem, vmem, vmem, vmem],
        out_specs=(vmem, vmem, vmem, vmem),
        scratch_shapes=[
            pltpu.VMEM((6, 10, 256, 256), BF16),
            pltpu.VMEM((6, 8, 256, 128), F32),
            pltpu.VMEM((6, 8, 256, 128), F32),
            pltpu.VMEM((6, 64, 128), F32),
            pltpu.VMEM((6, 1024, 256), BF16),
            pltpu.VMEM((6, 1024, 256), BF16),
            pltpu.VMEM((10, 256, 256), BF16),
            pltpu.VMEM((10, 128, 256), BF16),
            pltpu.VMEM((8, 256, 128), F32),
            pltpu.VMEM((8, 256, 128), F32),
            pltpu.VMEM((128, 128), F32),
            pltpu.VMEM((8, 128), jnp.int32),
            pltpu.VMEM((secs,) + own.shape, BF16),
            pltpu.VMEM((6, secs, TILES, 16, 128), BF16),
            pltpu.VMEM((6, secs, TILES, 16, 128), BF16),
            pltpu.VMEM((6, TILES, 16, 128), BF16),
            pltpu.VMEM((6, dps, TILES, 16, 128), BF16),
            pltpu.VMEM((6, TILES, 16, 128), BF16),
            pltpu.VMEM(images_in.shape, BF16),
            pltpu.VMEM(own.shape, F32),
            dma((2,)),
            dma((3, secs - 1)), dma((3, secs - 1)),
            dma((6, secs - 1)), dma((6, secs - 1)),
            dma((6, max(dps - 1, TILES))), dma((6, dps)),
            dma((6, dps)), dma((6, TILES)),
        ],
        compiler_params=pltpu.CompilerParams(
            vmem_limit_bytes=63 * 1024 * 1024 + 768 * 1024, collective_id=0, has_side_effects=True),
    )(images_in, labels, own, gain, bias, hw, hb)


def per_device(images_in, labels, conv_weight, frn_gain, frn_bias, head_weight, head_bias):
    images = images_in.shape[0]
    dps, secs = lax.axis_size("dp"), lax.axis_size("section")
    blocks, convs, depth, share = conv_weight.shape
    own = jnp.swapaxes(conv_weight, 2, 3).reshape(blocks * convs, share, depth)
    conv, norm, head, head_b = all_grads(
        images * dps * secs, dps, secs, images_in, labels.reshape(1, images), own, frn_gain,
        frn_bias, head_weight.T, head_bias.reshape(1, -1))
    return (jnp.swapaxes(conv.reshape(blocks, convs, share, depth), 2, 3), norm, head.T,
            head_b.reshape(-1))


def solution(mesh):
    return jax.shard_map(
        per_device,
        mesh=mesh,
        in_specs=(
            P(("dp", "section"), None),
            P(("dp", "section")),
            P(None, None, None, "section"),
            P(),
            P(),
            P(),
            P(),
        ),
        out_specs=(P(None, None, None, "section"), P(), P(), P()),
        check_vma=False,
    )
```

```python
import functools

import jax
import jax.numpy as jnp
from jax import lax
from jax.experimental import pallas as pl
from jax.experimental.pallas import tpu as pltpu
from jax.sharding import PartitionSpec as P

F32 = jnp.float32
BF16 = jnp.bfloat16
MESH = pl.DeviceIdType.MESH
eps = 1e-06
prior_precision = 0.5
OFFSETS = (0, 1, 2, -1)


TILES = 5
DIRECT = (1, 0)
AFTER = {3: (("b", 5),), 2: (("b", 4),), 1: (("b", 3),)}
TAIL = (("b", 2), ("c", 5), ("c", 4), ("b", 1), ("c", 3), ("b", 0), ("c", 2),
        ("f", 5), ("f", 4), ("f", 3), ("f", 2), ("f", 1), ("f", 0))


def owner(k, m, dps):
    return (m * dps // TILES + 3 * k) % dps


def kernel(total, dps, secs, img_hbm, labels, own_hbm, gain, bias, hw, hb,
           conv_out, norm_out, hw_out, hb_out,
           xs, zs, dsw, rs, wf, wb, qs, qt, du2, du1, hw2, lab, wt, buf, in_a, tot, in_b,
           fin, img, own, load, w_send, w_recv, a_send, a_recv, b_send, b_recv, c_send, c_recv):
    dp, sec = lax.axis_index("dp"), lax.axis_index("section")
    lane = lax.broadcasted_iota(jnp.int32, (1, 128), 1)
    low = lane < 64
    classes = hw.shape[0]

    load_own = pltpu.make_async_copy(own_hbm, own, load.at[0])
    load_img = pltpu.make_async_copy(img_hbm, img, load.at[1])
    load_own.start()
    load_img.start()
    barrier = pltpu.get_barrier_semaphore()
    for d in range(1, secs):
        pl.semaphore_signal(barrier, inc=1, device_id=(dp, lax.rem(sec + d, secs)),
                            device_id_type=MESH)

    def greet(d, carry):
        pl.semaphore_signal(barrier, inc=1, device_id=(lax.rem(dp + d, dps), sec),
                            device_id_type=MESH)
        return carry

    lax.fori_loop(1, dps, greet, 0)
    load_own.wait()
    wt[sec] = own[...].astype(BF16)
    pl.semaphore_wait(barrier, secs - 1 + dps - 1)

    def send_w(k, d):
        mine = wt.at[sec, k]
        return pltpu.make_async_remote_copy(
            src_ref=mine, dst_ref=mine, send_sem=w_send.at[k, d - 1],
            recv_sem=w_recv.at[k, d - 1], device_id=(dp, lax.rem(sec + d, secs)),
            device_id_type=MESH)

    def send_a(k, d):
        to = lax.rem(sec + d, secs)
        return pltpu.make_async_remote_copy(
            src_ref=buf.at[k, to], dst_ref=in_a.at[k, sec], send_sem=a_send.at[k, d - 1],
            recv_sem=a_recv.at[k, d - 1], device_id=(dp, to), device_id_type=MESH)

    def send_tile(k, m):
        to = owner(k, m, dps)
        return pltpu.make_async_remote_copy(
            src_ref=tot.at[k, m], dst_ref=in_b.at[k, dp, m], send_sem=b_send.at[k, m],
            recv_sem=b_recv.at[k, lax.rem(to - dp + dps - 1, dps)],
            device_id=(to, sec), device_id_type=MESH)

    def wait_tile(k, m, d):
        pltpu.make_async_remote_copy(
            src_ref=tot.at[k, m], dst_ref=in_b.at[k, lax.rem(dp - d + dps, dps), m],
            send_sem=b_send.at[k, m], recv_sem=b_recv.at[k, d - 1],
            device_id=(lax.rem(dp + d, dps), sec), device_id_type=MESH).wait_recv()

    def send_all(k, d):
        to = lax.rem(dp + d, dps)
        return pltpu.make_async_remote_copy(
            src_ref=tot.at[k], dst_ref=in_b.at[k, dp], send_sem=b_send.at[k, d - 1],
            recv_sem=b_recv.at[k, d - 1], device_id=(to, sec), device_id_type=MESH)

    def send_c(k, m, d):
        return pltpu.make_async_remote_copy(
            src_ref=fin.at[k, m], dst_ref=fin.at[k, m], send_sem=c_send.at[k, d - 1],
            recv_sem=c_recv.at[k, m], device_id=(lax.rem(dp + d, dps), sec),
            device_id_type=MESH)

    def each_dp(act):
        def step(d, carry):
            act(d)
            return carry
        lax.fori_loop(1, dps, step, 0)

    def resplit(v):
        whole = v[0:8] + v[8:16]
        top = whole.astype(BF16).astype(F32)
        return jnp.where(low, v, jnp.concatenate([top, whole - top], axis=0))

    def start_a(k):
        for d in range(1, secs):
            send_a(k, d).start()
        in_a[k, sec] = buf[k, sec]

    def start_b(k):
        for d in range(1, secs):
            send_a(k, d).wait_recv()
        for m in range(TILES):
            v = in_a[k, 0, m].astype(F32)
            for q in range(1, secs):
                v = v + in_a[k, q, m].astype(F32)
            tot[k, m] = (resplit(v) if m == TILES - 1 else v).astype(BF16)
        if k in DIRECT:
            each_dp(lambda d: send_all(k, d).start())
            in_b[k, dp] = tot[k]
            return
        for m in range(TILES):
            @pl.when(dp != owner(k, m, dps))
            def _():
                send_tile(k, m).start()

            @pl.when(dp == owner(k, m, dps))
            def _():
                in_b[k, dp, m] = tot[k, m]

    def sum_b(k, m):
        v = lax.fori_loop(1, dps, lambda p, acc: acc + in_b[k, p, m].astype(F32),
                          in_b[k, 0, m].astype(F32))
        fin[k, m] = (resplit(v) if m == TILES - 1 else v).astype(BF16)

    def start_c(k):
        for m in range(TILES):
            @pl.when(dp == owner(k, m, dps))
            def _():
                each_dp(lambda d: wait_tile(k, m, d))
                sum_b(k, m)
                each_dp(lambda d: send_c(k, m, d).start())

    def finish(k):
        if k in DIRECT:
            each_dp(lambda d: pltpu.make_async_remote_copy(
                src_ref=tot.at[k], dst_ref=in_b.at[k, lax.rem(dp - d + dps, dps)],
                send_sem=b_send.at[k, d - 1], recv_sem=b_recv.at[k, d - 1],
                device_id=(lax.rem(dp + d, dps), sec), device_id_type=MESH).wait_recv())
            for m in range(TILES):
                sum_b(k, m)
        else:
            for m in range(TILES):
                @pl.when(dp != owner(k, m, dps))
                def _():
                    send_c(k, m, 1).wait_recv()
        rows = [fin[k, m].astype(F32) for m in range(TILES)]
        side = pltpu.roll(rows[-1][0:8] + rows[-1][8:16], 64, 1)[:, 0:64]
        conv_out[k] = (jnp.concatenate(rows[:-1] + [rows[-1][:, 0:64]], axis=1)
                       + prior_precision * own[k])
        b, j = k // 2, k % 2
        norm_out[b, j, 0:1] = side[0:1] + prior_precision * gain[b, j:j + 1, :]
        norm_out[b, j, 1:2] = side[1:2] + prior_precision * bias[b, j:j + 1, :]
        if k == 5:
            hw_out[0:6] = side[2:8] + prior_precision * hw[0:6]
        if k == 4:
            hw_out[6:classes] = side[2:classes - 4] + prior_precision * hw[6:classes]
            hb_out[...] = side[6:7, 0:classes] + prior_precision * hb[...]

    for k in range(6):
        for d in range(1, secs):
            send_w(k, d).start()

    def both(v):
        return v + pltpu.roll(v, 64, 1)

    def twice(v):
        return jnp.concatenate([v, v], axis=1)

    for ref in (qs, qt):
        ref[0] = jnp.zeros(ref.shape[1:], BF16)
        ref[9] = jnp.zeros(ref.shape[1:], BF16)
    for k in range(6):
        xs[k, 0] = jnp.zeros((256, 256), BF16)
        xs[k, 9] = jnp.zeros((256, 256), BF16)

    def put(ref, y, v):
        edge = jnp.zeros((1, 64, 128), F32)
        after = jnp.concatenate([v[1:], edge], axis=0)
        before = jnp.concatenate([edge, v[:3]], axis=0)
        beside = jnp.where(low[None], after, before)
        ref[y + 1, :, 0:128] = v.reshape(256, 128).astype(BF16)
        ref[y + 1, :, 128:256] = beside.reshape(256, 128).astype(BF16)

    def conv(src, w, body, init):
        def run(*accs):
            for m in range(2):
                for kt in range(2):
                    at = (2 * m + kt) * 256
                    pltpu.matmul_push_rhs(w[at:at + 256, :], kt, m)
            for kt in range(2):
                for y2 in range(4):
                    for m in range(2):
                        pltpu.matmul_acc_lhs(accs[4 * m + y2], src[2 * y2 + 2 * m + kt],
                                             load_staged_rhs=kt if y2 == 0 else None)
            carry = init
            for y2 in range(4):
                out = pltpu.matmul_pop(accs[y2]) + pltpu.matmul_pop(accs[4 + y2])
                for yo in range(2):
                    carry = body(2 * y2 + yo, out[:, yo * 128:yo * 128 + 128], carry)
            return carry

        return pl.run_scoped(run, *[pltpu.ACC(m)((256, 256), F32) for m in range(2) for _ in range(4)])

    def split(v):
        top = v.astype(BF16)
        return [top, (v - top.astype(F32)).astype(BF16)]

    def dot_f32(a, b):
        def run(acc):
            half = jnp.concatenate(split(b), axis=1)
            pltpu.matmul_push_rhs(jnp.concatenate([half, half], axis=0), 0, 0)
            pltpu.matmul_acc_lhs(acc, jnp.concatenate(split(a), axis=1), load_staged_rhs=0)
            out = pltpu.matmul_pop(acc)
            return out[:, 0:128] + out[:, 128:256]

        return pl.run_scoped(run, pltpu.ACC(0)((a.shape[0], 256), F32))

    zero_sum = jnp.zeros((64, 128), F32)

    def over_pairs(v):
        return jnp.sum(v.reshape(4, 64, 128), axis=0)

    load_img.wait()
    for y in range(8):
        slab = jnp.stack([img[:, (y * 4 + j) * 128:(y * 4 + j + 1) * 128]
                          for j in range(4)], axis=0).astype(F32)
        put(xs.at[0], y, slab)

    def spread(k):
        b, j = k // 2, k % 2
        for d in range(1, secs):
            send_w(k, d).wait_recv()
        zero = jnp.zeros((64, 128), BF16)
        none = jnp.zeros((64, 128), F32)
        flat = jnp.concatenate([wt[q, k] for q in range(secs)], axis=0).astype(F32)
        wide = jnp.concatenate([none[:, 0:64], flat, none], axis=1)
        square = jnp.concatenate([flat, none[:, 0:64]], axis=1)
        cols = jnp.concatenate([square, square], axis=0).T
        plain = [cols[t * 64:(t + 1) * 64] for t in range(9)]
        for a in range(3):
            for s, xi in enumerate(OFFSETS):
                left = plain[a * 3 + xi + 1] if 0 <= xi + 1 <= 2 else none
                right = plain[a * 3 + xi] if 0 <= xi <= 2 else none
                tile = jnp.where(low, left, right).astype(BF16)
                at = ((2 - a) * 3 + 2 - xi) * 64
                back = wide[:, at:at + 128]
                if xi == -1:
                    back = jnp.where(low, back, 0.0)
                if xi == 2:
                    back = jnp.where(low, 0.0, back)
                back = back.astype(BF16)
                for yo in range(2):
                    row = (a + yo) * 256 + s * 64
                    wf[k, row:row + 64, yo * 128:yo * 128 + 128] = tile
                    if k > 0:
                        wb[k, row:row + 64, yo * 128:yo * 128 + 128] = back
        for ref in (wf, wb):
            for s in range(4):
                ref[k, 768 + s * 64:832 + s * 64, 0:128] = zero
                ref[k, s * 64:s * 64 + 64, 128:256] = zero

    pooled = zero_sum
    for k in range(6):
        b, j = k // 2, k % 2
        spread(k)

        def keep(y, out, energy):
            zs[k, y] = out
            return energy + over_pairs(out * out)

        energy = conv(xs.at[k], wf.at[k], keep, zero_sum)
        r = lax.rsqrt(both(energy) * (1.0 / 64) + eps)
        rs[k] = r
        scale = r * twice(gain[b, j:j + 1, :])
        shift = twice(bias[b, j:j + 1, :])

        def activate(y, carry):
            u = zs[k, y].reshape(4, 64, 128) * scale[None] + shift[None]
            if j == 1:
                u = u + xs[k - 1, y + 1, :, 0:128].astype(F32).reshape(4, 64, 128)
            sig = 0.5 * jnp.tanh(0.5 * u) + 0.5
            out = u * sig
            dsw[k, y] = (sig + out * (1.0 - sig)).reshape(256, 128)
            if k < 5:
                put(xs.at[k + 1], y, out)
                return carry
            return carry + jnp.sum(out.astype(BF16).astype(F32), axis=0)

        pooled = lax.fori_loop(0, 8, activate, pooled)

    pooled = both(pooled) * (1.0 / 64)
    hw2[...] = jnp.zeros((128, 128), F32)
    hw2[0:hw.shape[0], :] = twice(hw[...])
    lab[...] = jnp.zeros((8, 128), jnp.int32)
    lab[0:1, 0:64] = labels[...]
    hbias = jnp.concatenate([hb[...], jnp.zeros((1, 128 - classes), F32)], axis=1)
    logits = dot_f32(jnp.where(low, pooled, 0.0), hw2[...].T) + hbias
    live = lane < classes
    logits = jnp.where(live, logits, -1e30)
    top = jnp.max(logits, axis=1, keepdims=True)
    expo = jnp.where(live, jnp.exp(logits - top), 0.0)
    probs = expo / jnp.sum(expo, axis=1, keepdims=True)
    onehot = jnp.where(
        lax.broadcasted_iota(jnp.int32, (128, 128), 0) == lab[0:1, :], 1.0, 0.0).T
    dl = (probs - onehot[0:64]) * (1.0 / total)
    dlt = jnp.concatenate([dl, jnp.zeros((64, 128), F32)], axis=0).T
    tall = jnp.concatenate([pooled, jnp.zeros((64, 128), F32)], axis=0)
    d_head = dot_f32(dlt[0:16], tall)
    row = lax.broadcasted_iota(jnp.int32, (8, 128), 0)
    d_bias = pltpu.roll(jnp.sum(dl, axis=0, keepdims=True), 64, 1)
    head_rows = {
        5: jnp.where(row >= 2, pltpu.roll(d_head[0:8], 2, 0), 0.0),
        4: jnp.where(row == 6, d_bias,
                     jnp.where(row >= 4, pltpu.roll(d_head[8:16], 4, 0),
                               pltpu.roll(d_head[0:8], 4, 0))),
    }
    spread_g = dot_f32(dl, hw2[...]) * (1.0 / 64)
    spread_g = spread_g.astype(BF16).astype(F32)

    def advance(k):
        for act, other in AFTER.get(k, ()):
            {"b": start_b, "c": start_c}[act](other)

    def tally(k, y, d, sums):
        return (sums[0] + over_pairs(d * zs[k, y]), sums[1] + over_pairs(d))

    def begin(y, sums):
        d = (dsw[5, y].reshape(4, 64, 128) * spread_g[None]).reshape(256, 128)
        du2[y] = d
        return tally(5, y, d, sums)

    sums = lax.fori_loop(0, 8, begin, (zero_sum, zero_sum))
    for k in range(5, -1, -1):
        b, j = k // 2, k % 2
        source = du2 if j == 1 else du1
        r = rs[k]
        dg = both(sums[0]) * r
        db = both(sums[1])
        extra = jnp.where(row == 0, jnp.sum(dg, axis=0, keepdims=True),
                          jnp.where(row == 1, jnp.sum(db, axis=0, keepdims=True),
                                    head_rows.get(k, 0.0)))
        top = extra.astype(BF16).astype(F32)
        side = jnp.concatenate([top, extra - top] * secs, axis=0)
        c1 = r * twice(gain[b, j:j + 1, :])
        c2 = c1 * dg * r * (1.0 / 64)

        def settle(y, carry):
            d = (source[y].reshape(4, 64, 128) * c1[None]
                 - zs[k, y].reshape(4, 64, 128) * c2[None])
            if k > 0:
                put(qs, y, d)
            qt[y + 1] = d.reshape(256, 128).T.astype(BF16)
            return carry

        lax.fori_loop(0, 8, settle, 0, unroll=8)

        def weight_terms(*accs):
            for step in range(4):
                for m in range(2):
                    y = 2 * step + m
                    pltpu.matmul_push_rhs(xs[k, y + 1], step % 2, m)
                    for a in range(3):
                        pltpu.matmul_acc_lhs(accs[3 * m + a], qt[y - a + 2],
                                             load_staged_rhs=step % 2 if a == 0 else None)
            return jnp.concatenate(
                [pltpu.matmul_pop(accs[a]) + pltpu.matmul_pop(accs[3 + a]) for a in range(3)], axis=0)

        terms = pl.run_scoped(
            weight_terms, *[pltpu.ACC(m)((128, 256), F32) for m in range(2) for _ in range(3)])
        def rolled(a):
            return (pltpu.roll(terms[a * 128:a * 128 + 64], 64, 1)
                    + terms[a * 128 + 64:a * 128 + 128])

        first, last = rolled(0), rolled(2)
        swapped = jnp.concatenate([terms[128:192, 128:256], terms[128:192, 0:128]], axis=1)
        middle = swapped + pltpu.roll(terms[192:256], 64, 1)
        tiles = [first[:, 0:128], jnp.where(low, first[:, 128:256], middle[:, 0:128]),
                 middle[:, 128:256], last[:, 0:128], jnp.where(low, last[:, 128:256], side)]
        for m in range(TILES):
            v = tiles[m].astype(BF16)
            for q in range(secs):
                buf[k, q, m] = v[q * 16:q * 16 + 16]
        start_a(k)

        if j == 1:
            def to_first(y, out, sums):
                d = out * dsw[k - 1, y]
                du1[y] = d
                return tally(k - 1, y, d, sums)

            sums = conv(qs, wb.at[k], to_first, (zero_sum, zero_sum))
            advance(k)
        elif k > 0:
            def to_second(y, out, sums):
                g = (du2[y] + out).astype(BF16).astype(F32)
                d = g * dsw[k - 1, y]
                du2[y] = d
                return tally(k - 1, y, d, sums)

            sums = conv(qs, wb.at[k], to_second, (zero_sum, zero_sum))
            advance(k)

    for act, k in TAIL:
        {"b": start_b, "c": start_c, "f": finish}[act](k)
    for k in range(6):
        for d in range(1, secs):
            send_w(k, d).wait_send()
    for k in range(6):
        for d in range(1, secs):
            send_a(k, d).wait_send()
        if k in DIRECT:
            each_dp(lambda d: send_all(k, d).wait_send())
            continue
        for m in range(TILES):
            @pl.when(dp != owner(k, m, dps))
            def _():
                send_tile(k, m).wait_send()

            @pl.when(dp == owner(k, m, dps))
            def _():
                each_dp(lambda d: send_c(k, m, d).wait_send())


def all_grads(total, dps, secs, images_in, labels, own, gain, bias, hw, hb):
    vmem = pl.BlockSpec(memory_space=pltpu.VMEM)
    hbm = pl.BlockSpec(memory_space=pltpu.HBM)
    dma = pltpu.SemaphoreType.DMA
    return pl.pallas_call(
        functools.partial(kernel, total, dps, secs),
        out_shape=(jax.ShapeDtypeStruct(own.shape, F32),
                   jax.ShapeDtypeStruct(gain.shape[:2] + (2,) + gain.shape[2:], F32),
                   jax.ShapeDtypeStruct(hw.shape, F32),
                   jax.ShapeDtypeStruct(hb.shape, F32)),
        in_specs=[hbm, vmem, hbm, vmem, vmem, vmem, vmem],
        out_specs=(vmem, vmem, vmem, vmem),
        scratch_shapes=[
            pltpu.VMEM((6, 10, 256, 256), BF16),
            pltpu.VMEM((6, 8, 256, 128), F32),
            pltpu.VMEM((6, 8, 256, 128), F32),
            pltpu.VMEM((6, 64, 128), F32),
            pltpu.VMEM((6, 1024, 256), BF16),
            pltpu.VMEM((6, 1024, 256), BF16),
            pltpu.VMEM((10, 256, 256), BF16),
            pltpu.VMEM((10, 128, 256), BF16),
            pltpu.VMEM((8, 256, 128), F32),
            pltpu.VMEM((8, 256, 128), F32),
            pltpu.VMEM((128, 128), F32),
            pltpu.VMEM((8, 128), jnp.int32),
            pltpu.VMEM((secs,) + own.shape, BF16),
            pltpu.VMEM((6, secs, TILES, 16, 128), BF16),
            pltpu.VMEM((6, secs, TILES, 16, 128), BF16),
            pltpu.VMEM((6, TILES, 16, 128), BF16),
            pltpu.VMEM((6, dps, TILES, 16, 128), BF16),
            pltpu.VMEM((6, TILES, 16, 128), BF16),
            pltpu.VMEM(images_in.shape, BF16),
            pltpu.VMEM(own.shape, F32),
            dma((2,)),
            dma((6, secs - 1)), dma((6, secs - 1)),
            dma((6, secs - 1)), dma((6, secs - 1)),
            dma((6, max(dps - 1, TILES))), dma((6, dps)),
            dma((6, dps)), dma((6, TILES)),
        ],
        compiler_params=pltpu.CompilerParams(
            vmem_limit_bytes=63 * 1024 * 1024 + 768 * 1024, collective_id=0, has_side_effects=True),
    )(images_in, labels, own, gain, bias, hw, hb)


def hand_over(*refs):
    half = len(refs) // 2
    for i in range(half):
        refs[half + i][...] = refs[i][...]


def outputs(*arrays):
    vmem = pl.BlockSpec(memory_space=pltpu.VMEM)
    return pl.pallas_call(
        hand_over,
        out_shape=tuple(jax.ShapeDtypeStruct(v.shape, v.dtype) for v in arrays),
        in_specs=[vmem] * len(arrays),
        out_specs=(vmem,) * len(arrays),
    )(*arrays)


def per_device(images_in, labels, conv_weight, frn_gain, frn_bias, head_weight, head_bias):
    images = images_in.shape[0]
    dps, secs = lax.axis_size("dp"), lax.axis_size("section")
    blocks, convs, depth, share = conv_weight.shape
    own = jnp.swapaxes(conv_weight, 2, 3).reshape(blocks * convs, share, depth)
    conv, norm, head, head_b = outputs(*all_grads(
        images * dps * secs, dps, secs, images_in, labels.reshape(1, images), own, frn_gain,
        frn_bias, head_weight.T, head_bias.reshape(1, -1)))
    return (jnp.swapaxes(conv.reshape(blocks, convs, share, depth), 2, 3), norm, head.T,
            head_b.reshape(-1))


def solution(mesh):
    return jax.shard_map(
        per_device,
        mesh=mesh,
        in_specs=(
            P(("dp", "section"), None),
            P(("dp", "section")),
            P(None, None, None, "section"),
            P(),
            P(),
            P(),
            P(),
        ),
        out_specs=(P(None, None, None, "section"), P(), P(), P()),
        check_vma=False,
    )
```

```python
import functools

import jax
import jax.numpy as jnp
from jax import lax
from jax.experimental import pallas as pl
from jax.experimental.pallas import tpu as pltpu
from jax.sharding import PartitionSpec as P

F32 = jnp.float32
BF16 = jnp.bfloat16
MESH = pl.DeviceIdType.MESH
eps = 1e-06
prior_precision = 0.5
OFFSETS = (0, 1, 2, -1)


TILES = 5
AFTER = {1: (("b", 5),)}
TAIL = (("b", 4), ("b", 3), ("b", 2), ("b", 1), ("f", 5), ("b", 0), ("f", 4), ("f", 3),
        ("f", 2), ("f", 1), ("f", 0))


def kernel(total, dps, secs, img_hbm, labels, own_hbm, gain, bias, hw, hb,
           conv_out, norm_out, hw_out, hb_out,
           xs, zs, dsw, rs, wf, wb, qs, qt, du2, du1, hw2, lab, wt, buf, in_a, in_b, img, own, load, w_send, w_recv, a_send, a_recv, b_send, b_recv):
    dp, sec = lax.axis_index("dp"), lax.axis_index("section")
    lane = lax.broadcasted_iota(jnp.int32, (1, 128), 1)
    low = lane < 64
    classes = hw.shape[0]
    pair = 2 if dps % 2 == 0 else 1
    group, rows_of = pair * secs, dps // pair
    line, side_of = dp // pair, lax.rem(dp, pair)
    mine = side_of * secs + sec

    def each(n, act):
        def step(d, carry):
            act(d)
            return carry
        lax.fori_loop(1, n, step, 0)

    load_own = pltpu.make_async_copy(own_hbm, own, load.at[0])
    load_img = pltpu.make_async_copy(img_hbm, img, load.at[1])
    load_own.start()
    load_img.start()
    barrier = pltpu.get_barrier_semaphore()
    for d in range(1, group):
        to = lax.rem(mine + d, group)
        pl.semaphore_signal(barrier, inc=1,
                            device_id=(line * pair + to // secs, lax.rem(to, secs)),
                            device_id_type=MESH)
    each(rows_of, lambda d: pl.semaphore_signal(
        barrier, inc=1, device_id=(lax.rem(line + d, rows_of) * pair + side_of, sec),
        device_id_type=MESH))
    load_own.wait()
    wt[sec] = own[...].astype(BF16)
    pl.semaphore_wait(barrier, group - 1 + rows_of - 1)

    def send_w(k, d):
        mine = wt.at[sec, k]
        return pltpu.make_async_remote_copy(
            src_ref=mine, dst_ref=mine, send_sem=w_send.at[k, d - 1],
            recv_sem=w_recv.at[k, d - 1], device_id=(dp, lax.rem(sec + d, secs)),
            device_id_type=MESH)

    def send_a(k, d):
        to = lax.rem(mine + d, group)
        return pltpu.make_async_remote_copy(
            src_ref=buf.at[k, lax.rem(to, secs)], dst_ref=in_a.at[k, mine],
            send_sem=a_send.at[k, d - 1], recv_sem=a_recv.at[k, d - 1],
            device_id=(line * pair + to // secs, lax.rem(to, secs)), device_id_type=MESH)

    def wait_a(k, d):
        to = lax.rem(mine + d, group)
        pltpu.make_async_remote_copy(
            src_ref=buf.at[k, lax.rem(to, secs)], dst_ref=in_a.at[k, lax.rem(mine + group - d, group)],
            send_sem=a_send.at[k, d - 1], recv_sem=a_recv.at[k, d - 1],
            device_id=(line * pair + to // secs, lax.rem(to, secs)),
            device_id_type=MESH).wait_recv()

    def send_b(k, d, slot):
        to = lax.rem(line + d, rows_of)
        return pltpu.make_async_remote_copy(
            src_ref=in_b.at[k, line], dst_ref=in_b.at[k, slot], send_sem=b_send.at[k, d - 1],
            recv_sem=b_recv.at[k, d - 1], device_id=(to * pair + side_of, sec),
            device_id_type=MESH)

    def resplit(v):
        whole = v[0:8] + v[8:16]
        top = whole.astype(BF16).astype(F32)
        return jnp.where(low, v, jnp.concatenate([top, whole - top], axis=0))

    def start_a(k):
        for d in range(1, group):
            send_a(k, d).start()
        in_a[k, mine] = buf[k, sec]

    def add_up(ref, k, m, n):
        v = ref[k, 0, m].astype(F32)
        if n <= 8:
            for p in range(1, n):
                v = v + ref[k, p, m].astype(F32)
            return v
        return lax.fori_loop(1, n, lambda p, acc: acc + ref[k, p, m].astype(F32), v)

    def start_b(k):
        for d in range(1, group):
            wait_a(k, d)
        for m in range(TILES):
            v = add_up(in_a, k, m, group)
            in_b[k, line, m] = (resplit(v) if m == TILES - 1 else v).astype(BF16)
        each(rows_of, lambda d: send_b(k, d, line).start())

    def finish(k):
        each(rows_of, lambda d: send_b(k, d, lax.rem(line + rows_of - d, rows_of)).wait_recv())
        rows = [add_up(in_b, k, m, rows_of) for m in range(TILES)]
        side = pltpu.roll(rows[-1][0:8] + rows[-1][8:16], 64, 1)[:, 0:64]
        conv_out[k] = (jnp.concatenate(rows[:-1] + [rows[-1][:, 0:64]], axis=1)
                       + prior_precision * own[k])
        b, j = k // 2, k % 2
        norm_out[b, j, 0:1] = side[0:1] + prior_precision * gain[b, j:j + 1, :]
        norm_out[b, j, 1:2] = side[1:2] + prior_precision * bias[b, j:j + 1, :]
        if k == 5:
            hw_out[0:6] = side[2:8] + prior_precision * hw[0:6]
        if k == 4:
            hw_out[6:classes] = side[2:classes - 4] + prior_precision * hw[6:classes]
            hb_out[...] = side[6:7, 0:classes] + prior_precision * hb[...]

    for k in range(6):
        for d in range(1, secs):
            send_w(k, d).start()

    def both(v):
        return v + pltpu.roll(v, 64, 1)

    def twice(v):
        return jnp.concatenate([v, v], axis=1)

    for ref in (qs, qt):
        ref[0] = jnp.zeros(ref.shape[1:], BF16)
        ref[9] = jnp.zeros(ref.shape[1:], BF16)
    for k in range(6):
        xs[k, 0] = jnp.zeros((256, 256), BF16)
        xs[k, 9] = jnp.zeros((256, 256), BF16)

    def put(ref, y, v):
        edge = jnp.zeros((1, 64, 128), F32)
        after = jnp.concatenate([v[1:], edge], axis=0)
        before = jnp.concatenate([edge, v[:3]], axis=0)
        beside = jnp.where(low[None], after, before)
        ref[y + 1, :, 0:128] = v.reshape(256, 128).astype(BF16)
        ref[y + 1, :, 128:256] = beside.reshape(256, 128).astype(BF16)

    def conv(src, w, body, init):
        def run(*accs):
            for m in range(2):
                for kt in range(2):
                    at = (2 * m + kt) * 256
                    pltpu.matmul_push_rhs(w[at:at + 256, :], kt, m)
            for kt in range(2):
                for y2 in range(4):
                    for m in range(2):
                        pltpu.matmul_acc_lhs(accs[4 * m + y2], src[2 * y2 + 2 * m + kt],
                                             load_staged_rhs=kt if y2 == 0 else None)
            carry = init
            for y2 in range(4):
                out = pltpu.matmul_pop(accs[y2]) + pltpu.matmul_pop(accs[4 + y2])
                for yo in range(2):
                    carry = body(2 * y2 + yo, out[:, yo * 128:yo * 128 + 128], carry)
            return carry

        return pl.run_scoped(run, *[pltpu.ACC(m)((256, 256), F32) for m in range(2) for _ in range(4)])

    def split(v):
        top = v.astype(BF16)
        return [top, (v - top.astype(F32)).astype(BF16)]

    def dot_f32(a, b):
        def run(acc):
            half = jnp.concatenate(split(b), axis=1)
            pltpu.matmul_push_rhs(jnp.concatenate([half, half], axis=0), 0, 0)
            pltpu.matmul_acc_lhs(acc, jnp.concatenate(split(a), axis=1), load_staged_rhs=0)
            out = pltpu.matmul_pop(acc)
            return out[:, 0:128] + out[:, 128:256]

        return pl.run_scoped(run, pltpu.ACC(0)((a.shape[0], 256), F32))

    zero_sum = jnp.zeros((64, 128), F32)

    def over_pairs(v):
        return jnp.sum(v.reshape(4, 64, 128), axis=0)

    load_img.wait()
    for y in range(8):
        slab = jnp.stack([img[:, (y * 4 + j) * 128:(y * 4 + j + 1) * 128]
                          for j in range(4)], axis=0).astype(F32)
        put(xs.at[0], y, slab)

    def spread(k):
        b, j = k // 2, k % 2
        for d in range(1, secs):
            send_w(k, d).wait_recv()
        zero = jnp.zeros((64, 128), BF16)
        none = jnp.zeros((64, 128), F32)
        flat = jnp.concatenate([wt[q, k] for q in range(secs)], axis=0).astype(F32)
        wide = jnp.concatenate([none[:, 0:64], flat, none], axis=1)
        square = jnp.concatenate([flat, none[:, 0:64]], axis=1)
        cols = jnp.concatenate([square, square], axis=0).T
        plain = [cols[t * 64:(t + 1) * 64] for t in range(9)]
        for a in range(3):
            for s, xi in enumerate(OFFSETS):
                left = plain[a * 3 + xi + 1] if 0 <= xi + 1 <= 2 else none
                right = plain[a * 3 + xi] if 0 <= xi <= 2 else none
                tile = jnp.where(low, left, right).astype(BF16)
                at = ((2 - a) * 3 + 2 - xi) * 64
                back = wide[:, at:at + 128]
                if xi == -1:
                    back = jnp.where(low, back, 0.0)
                if xi == 2:
                    back = jnp.where(low, 0.0, back)
                back = back.astype(BF16)
                for yo in range(2):
                    row = (a + yo) * 256 + s * 64
                    wf[k, row:row + 64, yo * 128:yo * 128 + 128] = tile
                    if k > 0:
                        wb[k, row:row + 64, yo * 128:yo * 128 + 128] = back
        for ref in (wf, wb):
            for s in range(4):
                ref[k, 768 + s * 64:832 + s * 64, 0:128] = zero
                ref[k, s * 64:s * 64 + 64, 128:256] = zero

    pooled = zero_sum
    for k in range(6):
        b, j = k // 2, k % 2
        if k == 0:
            spread(0)

        def keep(y, out, energy):
            zs[k, y] = out
            return energy + over_pairs(out * out)

        energy = conv(xs.at[k], wf.at[k], keep, zero_sum)
        r = lax.rsqrt(both(energy) * (1.0 / 64) + eps)
        rs[k] = r
        scale = r * twice(gain[b, j:j + 1, :])
        shift = twice(bias[b, j:j + 1, :])

        def activate(y, carry):
            u = zs[k, y].reshape(4, 64, 128) * scale[None] + shift[None]
            if j == 1:
                u = u + xs[k - 1, y + 1, :, 0:128].astype(F32).reshape(4, 64, 128)
            sig = 0.5 * jnp.tanh(0.5 * u) + 0.5
            out = u * sig
            dsw[k, y] = (sig + out * (1.0 - sig)).reshape(256, 128)
            if k < 5:
                put(xs.at[k + 1], y, out)
                return carry
            return carry + jnp.sum(out.astype(BF16).astype(F32), axis=0)

        if k < 5:
            spread(k + 1)
        pooled = lax.fori_loop(0, 8, activate, pooled, unroll=8)

    pooled = both(pooled) * (1.0 / 64)
    hw2[...] = jnp.zeros((128, 128), F32)
    hw2[0:hw.shape[0], :] = twice(hw[...])
    lab[...] = jnp.zeros((8, 128), jnp.int32)
    lab[0:1, 0:64] = labels[...]
    hbias = jnp.concatenate([hb[...], jnp.zeros((1, 128 - classes), F32)], axis=1)
    logits = dot_f32(jnp.where(low, pooled, 0.0), hw2[...].T) + hbias
    live = lane < classes
    logits = jnp.where(live, logits, -1e30)
    top = jnp.max(logits, axis=1, keepdims=True)
    expo = jnp.where(live, jnp.exp(logits - top), 0.0)
    probs = expo / jnp.sum(expo, axis=1, keepdims=True)
    onehot = jnp.where(
        lax.broadcasted_iota(jnp.int32, (128, 128), 0) == lab[0:1, :], 1.0, 0.0).T
    dl = (probs - onehot[0:64]) * (1.0 / total)
    dlt = jnp.concatenate([dl, jnp.zeros((64, 128), F32)], axis=0).T
    tall = jnp.concatenate([pooled, jnp.zeros((64, 128), F32)], axis=0)
    d_head = dot_f32(dlt[0:16], tall)
    row = lax.broadcasted_iota(jnp.int32, (8, 128), 0)
    d_bias = pltpu.roll(jnp.sum(dl, axis=0, keepdims=True), 64, 1)
    head_rows = {
        5: jnp.where(row >= 2, pltpu.roll(d_head[0:8], 2, 0), 0.0),
        4: jnp.where(row == 6, d_bias,
                     jnp.where(row >= 4, pltpu.roll(d_head[8:16], 4, 0),
                               pltpu.roll(d_head[0:8], 4, 0))),
    }
    spread_g = dot_f32(dl, hw2[...]) * (1.0 / 64)
    spread_g = spread_g.astype(BF16).astype(F32)

    def advance(k):
        for act, other in AFTER.get(k, ()):
            {"b": start_b, "f": finish}[act](other)

    def tally(k, y, d, sums):
        return (sums[0] + over_pairs(d * zs[k, y]), sums[1] + over_pairs(d))

    def begin(y, sums):
        d = (dsw[5, y].reshape(4, 64, 128) * spread_g[None]).reshape(256, 128)
        du2[y] = d
        return tally(5, y, d, sums)

    sums = lax.fori_loop(0, 8, begin, (zero_sum, zero_sum))
    for k in range(5, -1, -1):
        b, j = k // 2, k % 2
        source = du2 if j == 1 else du1
        r = rs[k]
        dg = both(sums[0]) * r
        db = both(sums[1])
        extra = jnp.where(row == 0, jnp.sum(dg, axis=0, keepdims=True),
                          jnp.where(row == 1, jnp.sum(db, axis=0, keepdims=True),
                                    head_rows.get(k, 0.0)))
        top = extra.astype(BF16).astype(F32)
        side = jnp.concatenate([top, extra - top] * secs, axis=0)
        c1 = r * twice(gain[b, j:j + 1, :])
        c2 = c1 * dg * r * (1.0 / 64)

        def settle(y, carry):
            d = (source[y].reshape(4, 64, 128) * c1[None]
                 - zs[k, y].reshape(4, 64, 128) * c2[None])
            if k > 0:
                put(qs, y, d)
            qt[y + 1] = d.reshape(256, 128).T.astype(BF16)
            return carry

        lax.fori_loop(0, 8, settle, 0, unroll=8)

        def weight_terms(*accs):
            for step in range(4):
                for m in range(2):
                    y = 2 * step + m
                    pltpu.matmul_push_rhs(xs[k, y + 1], step % 2, m)
                    for a in range(3):
                        pltpu.matmul_acc_lhs(accs[3 * m + a], qt[y - a + 2],
                                             load_staged_rhs=step % 2 if a == 0 else None)
            return jnp.concatenate(
                [pltpu.matmul_pop(accs[a]) + pltpu.matmul_pop(accs[3 + a]) for a in range(3)], axis=0)

        terms = pl.run_scoped(
            weight_terms, *[pltpu.ACC(m)((128, 256), F32) for m in range(2) for _ in range(3)])
        def rolled(a):
            return (pltpu.roll(terms[a * 128:a * 128 + 64], 64, 1)
                    + terms[a * 128 + 64:a * 128 + 128])

        first, last = rolled(0), rolled(2)
        swapped = jnp.concatenate([terms[128:192, 128:256], terms[128:192, 0:128]], axis=1)
        middle = swapped + pltpu.roll(terms[192:256], 64, 1)
        tiles = [first[:, 0:128], jnp.where(low, first[:, 128:256], middle[:, 0:128]),
                 middle[:, 128:256], last[:, 0:128], jnp.where(low, last[:, 128:256], side)]
        for m in range(TILES):
            v = tiles[m].astype(BF16)
            for q in range(secs):
                buf[k, q, m] = v[q * 16:q * 16 + 16]
        start_a(k)

        if j == 1:
            def to_first(y, out, sums):
                d = out * dsw[k - 1, y]
                du1[y] = d
                return tally(k - 1, y, d, sums)

            sums = conv(qs, wb.at[k], to_first, (zero_sum, zero_sum))
            advance(k)
        elif k > 0:
            def to_second(y, out, sums):
                g = (du2[y] + out).astype(BF16).astype(F32)
                d = g * dsw[k - 1, y]
                du2[y] = d
                return tally(k - 1, y, d, sums)

            sums = conv(qs, wb.at[k], to_second, (zero_sum, zero_sum))
            advance(k)

    for act, k in TAIL:
        {"b": start_b, "f": finish}[act](k)
    for k in range(6):
        for d in range(1, secs):
            send_w(k, d).wait_send()
    for k in range(6):
        for d in range(1, group):
            send_a(k, d).wait_send()
        each(rows_of, lambda d: send_b(k, d, line).wait_send())


def all_grads(total, dps, secs, images_in, labels, own, gain, bias, hw, hb):
    vmem = pl.BlockSpec(memory_space=pltpu.VMEM)
    hbm = pl.BlockSpec(memory_space=pltpu.HBM)
    dma = pltpu.SemaphoreType.DMA
    pair = 2 if dps % 2 == 0 else 1
    group = pair * secs
    return pl.pallas_call(
        functools.partial(kernel, total, dps, secs),
        out_shape=(jax.ShapeDtypeStruct(own.shape, F32),
                   jax.ShapeDtypeStruct(gain.shape[:2] + (2,) + gain.shape[2:], F32),
                   jax.ShapeDtypeStruct(hw.shape, F32),
                   jax.ShapeDtypeStruct(hb.shape, F32)),
        in_specs=[hbm, vmem, hbm, vmem, vmem, vmem, vmem],
        out_specs=(vmem, vmem, vmem, vmem),
        scratch_shapes=[
            pltpu.VMEM((6, 10, 256, 256), BF16),
            pltpu.VMEM((6, 8, 256, 128), F32),
            pltpu.VMEM((6, 8, 256, 128), F32),
            pltpu.VMEM((6, 64, 128), F32),
            pltpu.VMEM((6, 1024, 256), BF16),
            pltpu.VMEM((6, 1024, 256), BF16),
            pltpu.VMEM((10, 256, 256), BF16),
            pltpu.VMEM((10, 128, 256), BF16),
            pltpu.VMEM((8, 256, 128), F32),
            pltpu.VMEM((8, 256, 128), F32),
            pltpu.VMEM((128, 128), F32),
            pltpu.VMEM((8, 128), jnp.int32),
            pltpu.VMEM((secs,) + own.shape, BF16),
            pltpu.VMEM((6, secs, TILES, 16, 128), BF16),
            pltpu.VMEM((6, group, TILES, 16, 128), BF16),
            pltpu.VMEM((6, dps // pair, TILES, 16, 128), BF16),
            pltpu.VMEM(images_in.shape, BF16),
            pltpu.VMEM(own.shape, F32),
            dma((2,)),
            dma((6, secs - 1)), dma((6, secs - 1)),
            dma((6, group - 1)), dma((6, group - 1)),
            dma((6, dps // pair - 1)), dma((6, dps // pair - 1)),
        ],
        compiler_params=pltpu.CompilerParams(
            vmem_limit_bytes=63 * 1024 * 1024 + 768 * 1024, collective_id=0, has_side_effects=True),
    )(images_in, labels, own, gain, bias, hw, hb)


def hand_over(*refs):
    half = len(refs) // 2
    for i in range(half):
        refs[half + i][...] = refs[i][...]


def outputs(*arrays):
    vmem = pl.BlockSpec(memory_space=pltpu.VMEM)
    return pl.pallas_call(
        hand_over,
        out_shape=tuple(jax.ShapeDtypeStruct(v.shape, v.dtype) for v in arrays),
        in_specs=[vmem] * len(arrays),
        out_specs=(vmem,) * len(arrays),
    )(*arrays)


def per_device(images_in, labels, conv_weight, frn_gain, frn_bias, head_weight, head_bias):
    images = images_in.shape[0]
    dps, secs = lax.axis_size("dp"), lax.axis_size("section")
    blocks, convs, depth, share = conv_weight.shape
    own = jnp.swapaxes(conv_weight, 2, 3).reshape(blocks * convs, share, depth)
    conv, norm, head, head_b = outputs(*all_grads(
        images * dps * secs, dps, secs, images_in, labels.reshape(1, images), own, frn_gain,
        frn_bias, head_weight.T, head_bias.reshape(1, -1)))
    return (jnp.swapaxes(conv.reshape(blocks, convs, share, depth), 2, 3), norm, head.T,
            head_b.reshape(-1))


def solution(mesh):
    return jax.shard_map(
        per_device,
        mesh=mesh,
        in_specs=(
            P(("dp", "section"), None),
            P(("dp", "section")),
            P(None, None, None, "section"),
            P(),
            P(),
            P(),
            P(),
        ),
        out_specs=(P(None, None, None, "section"), P(), P(), P()),
        check_vma=False,
    )
```

```python
import functools

import jax
import jax.numpy as jnp
from jax import lax
from jax.experimental import pallas as pl
from jax.experimental.pallas import tpu as pltpu
from jax.sharding import PartitionSpec as P

F32 = jnp.float32
BF16 = jnp.bfloat16
MESH = pl.DeviceIdType.MESH
eps = 1e-06
prior_precision = 0.5
OFFSETS = (0, 1, 2, -1)


TILES = 5
AFTER = {2: (("b", 5),), 1: (("b", 4),)}
TAIL = (("b", 3), ("b", 2), ("b", 1), ("f", 5), ("b", 0), ("f", 4), ("f", 3), ("f", 2), ("f", 1), ("f", 0))


def kernel(total, dps, secs, img_hbm, labels, own_hbm, gain, bias, hw, hb,
           conv_out, norm_out, hw_out, hb_out,
           xs, zs, dsw, rs, wf, wb, qs, qt, du2, du1, hw2, lab, wt, buf, in_a, in_b, img, own, load, w_send, w_recv, a_send, a_recv, b_send, b_recv):
    dp, sec = lax.axis_index("dp"), lax.axis_index("section")
    lane = lax.broadcasted_iota(jnp.int32, (1, 128), 1)
    low = lane < 64
    classes = hw.shape[0]
    pair = 2 if dps % 2 == 0 else 1
    group, rows_of = pair * secs, dps // pair
    line, side_of = dp // pair, lax.rem(dp, pair)
    mine = side_of * secs + sec

    def each(n, act):
        def step(d, carry):
            act(d)
            return carry
        lax.fori_loop(1, n, step, 0)

    load_own = pltpu.make_async_copy(own_hbm, own, load.at[0])
    load_img = pltpu.make_async_copy(img_hbm, img, load.at[1])
    load_own.start()
    load_img.start()
    barrier = pltpu.get_barrier_semaphore()
    for d in range(1, group):
        to = lax.rem(mine + d, group)
        pl.semaphore_signal(barrier, inc=1,
                            device_id=(line * pair + to // secs, lax.rem(to, secs)),
                            device_id_type=MESH)
    each(rows_of, lambda d: pl.semaphore_signal(
        barrier, inc=1, device_id=(lax.rem(line + d, rows_of) * pair + side_of, sec),
        device_id_type=MESH))
    load_own.wait()
    wt[sec] = own[...].astype(BF16)
    pl.semaphore_wait(barrier, group - 1 + rows_of - 1)

    def send_w(k, d):
        mine = wt.at[sec, k]
        return pltpu.make_async_remote_copy(
            src_ref=mine, dst_ref=mine, send_sem=w_send.at[k, d - 1],
            recv_sem=w_recv.at[k, d - 1], device_id=(dp, lax.rem(sec + d, secs)),
            device_id_type=MESH)

    def send_a(k, d):
        to = lax.rem(mine + d, group)
        return pltpu.make_async_remote_copy(
            src_ref=buf.at[k, lax.rem(to, secs)], dst_ref=in_a.at[k, mine],
            send_sem=a_send.at[k, d - 1], recv_sem=a_recv.at[k, d - 1],
            device_id=(line * pair + to // secs, lax.rem(to, secs)), device_id_type=MESH)

    def wait_a(k, d):
        to = lax.rem(mine + d, group)
        pltpu.make_async_remote_copy(
            src_ref=buf.at[k, lax.rem(to, secs)], dst_ref=in_a.at[k, lax.rem(mine + group - d, group)],
            send_sem=a_send.at[k, d - 1], recv_sem=a_recv.at[k, d - 1],
            device_id=(line * pair + to // secs, lax.rem(to, secs)),
            device_id_type=MESH).wait_recv()

    def send_b(k, d, slot):
        to = lax.rem(line + d, rows_of)
        return pltpu.make_async_remote_copy(
            src_ref=in_b.at[k, line], dst_ref=in_b.at[k, slot], send_sem=b_send.at[k, d - 1],
            recv_sem=b_recv.at[k, d - 1], device_id=(to * pair + side_of, sec),
            device_id_type=MESH)

    def resplit(v):
        whole = v[0:8] + v[8:16]
        top = whole.astype(BF16).astype(F32)
        return jnp.where(low, v, jnp.concatenate([top, whole - top], axis=0))

    def start_a(k):
        for d in range(1, group):
            send_a(k, d).start()
        in_a[k, mine] = buf[k, sec]

    def add_up(ref, k, m, n):
        v = ref[k, 0, m].astype(F32)
        if n <= 8:
            for p in range(1, n):
                v = v + ref[k, p, m].astype(F32)
            return v
        return lax.fori_loop(1, n, lambda p, acc: acc + ref[k, p, m].astype(F32), v)

    def start_b(k):
        for d in range(1, group):
            wait_a(k, d)
        for m in range(TILES):
            v = add_up(in_a, k, m, group)
            in_b[k, line, m] = (resplit(v) if m == TILES - 1 else v).astype(BF16)
        each(rows_of, lambda d: send_b(k, d, line).start())

    def finish(k):
        each(rows_of, lambda d: send_b(k, d, lax.rem(line + rows_of - d, rows_of)).wait_recv())
        rows = [add_up(in_b, k, m, rows_of) for m in range(TILES)]
        side = pltpu.roll(rows[-1][0:8] + rows[-1][8:16], 64, 1)[:, 0:64]
        conv_out[k] = (jnp.concatenate(rows[:-1] + [rows[-1][:, 0:64]], axis=1)
                       + prior_precision * own[k])
        b, j = k // 2, k % 2
        norm_out[b, j, 0:1] = side[0:1] + prior_precision * gain[b, j:j + 1, :]
        norm_out[b, j, 1:2] = side[1:2] + prior_precision * bias[b, j:j + 1, :]
        if k == 5:
            hw_out[0:6] = side[2:8] + prior_precision * hw[0:6]
        if k == 4:
            hw_out[6:classes] = side[2:classes - 4] + prior_precision * hw[6:classes]
            hb_out[...] = side[6:7, 0:classes] + prior_precision * hb[...]

    for k in range(6):
        for d in range(1, secs):
            send_w(k, d).start()

    def both(v):
        return v + pltpu.roll(v, 64, 1)

    def twice(v):
        return jnp.concatenate([v, v], axis=1)

    for ref in (qs, qt):
        ref[0] = jnp.zeros(ref.shape[1:], BF16)
        ref[9] = jnp.zeros(ref.shape[1:], BF16)
    for k in range(6):
        xs[k, 0] = jnp.zeros((256, 256), BF16)
        xs[k, 9] = jnp.zeros((256, 256), BF16)

    def put(ref, y, v):
        edge = jnp.zeros((1, 64, 128), F32)
        after = jnp.concatenate([v[1:], edge], axis=0)
        before = jnp.concatenate([edge, v[:3]], axis=0)
        beside = jnp.where(low[None], after, before)
        ref[y + 1, :, 0:128] = v.reshape(256, 128).astype(BF16)
        ref[y + 1, :, 128:256] = beside.reshape(256, 128).astype(BF16)

    def conv(src, w, body, init):
        def run(*accs):
            for m in range(2):
                for kt in range(2):
                    at = (2 * m + kt) * 256
                    pltpu.matmul_push_rhs(w[at:at + 256, :], kt, m)
            for kt in range(2):
                for y2 in range(4):
                    for m in range(2):
                        pltpu.matmul_acc_lhs(accs[4 * m + y2], src[2 * y2 + 2 * m + kt],
                                             load_staged_rhs=kt if y2 == 0 else None)
            carry = init
            for y2 in range(4):
                out = pltpu.matmul_pop(accs[y2]) + pltpu.matmul_pop(accs[4 + y2])
                for yo in range(2):
                    carry = body(2 * y2 + yo, out[:, yo * 128:yo * 128 + 128], carry)
            return carry

        return pl.run_scoped(run, *[pltpu.ACC(m)((256, 256), F32) for m in range(2) for _ in range(4)])

    def split(v):
        top = v.astype(BF16)
        return [top, (v - top.astype(F32)).astype(BF16)]

    def dot_f32(a, b):
        def run(acc):
            half = jnp.concatenate(split(b), axis=1)
            pltpu.matmul_push_rhs(jnp.concatenate([half, half], axis=0), 0, 0)
            pltpu.matmul_acc_lhs(acc, jnp.concatenate(split(a), axis=1), load_staged_rhs=0)
            out = pltpu.matmul_pop(acc)
            return out[:, 0:128] + out[:, 128:256]

        return pl.run_scoped(run, pltpu.ACC(0)((a.shape[0], 256), F32))

    zero_sum = jnp.zeros((64, 128), F32)

    def over_pairs(v):
        return jnp.sum(v.reshape(4, 64, 128), axis=0)

    load_img.wait()
    for y in range(8):
        slab = jnp.stack([img[:, (y * 4 + j) * 128:(y * 4 + j + 1) * 128]
                          for j in range(4)], axis=0).astype(F32)
        put(xs.at[0], y, slab)

    def spread(k):
        b, j = k // 2, k % 2
        for d in range(1, secs):
            send_w(k, d).wait_recv()
        zero = jnp.zeros((64, 128), BF16)
        none = jnp.zeros((64, 128), F32)
        flat = jnp.concatenate([wt[q, k] for q in range(secs)], axis=0).astype(F32)
        wide = jnp.concatenate([none[:, 0:64], flat, none], axis=1)
        square = jnp.concatenate([flat, none[:, 0:64]], axis=1)
        cols = jnp.concatenate([square, square], axis=0).T
        plain = [cols[t * 64:(t + 1) * 64] for t in range(9)]
        for a in range(3):
            for s, xi in enumerate(OFFSETS):
                left = plain[a * 3 + xi + 1] if 0 <= xi + 1 <= 2 else none
                right = plain[a * 3 + xi] if 0 <= xi <= 2 else none
                tile = jnp.where(low, left, right).astype(BF16)
                at = ((2 - a) * 3 + 2 - xi) * 64
                back = wide[:, at:at + 128]
                if xi == -1:
                    back = jnp.where(low, back, 0.0)
                if xi == 2:
                    back = jnp.where(low, 0.0, back)
                back = back.astype(BF16)
                for yo in range(2):
                    row = (a + yo) * 256 + s * 64
                    wf[k, row:row + 64, yo * 128:yo * 128 + 128] = tile
                    if k > 0:
                        wb[k, row:row + 64, yo * 128:yo * 128 + 128] = back
        for ref in (wf, wb):
            for s in range(4):
                ref[k, 768 + s * 64:832 + s * 64, 0:128] = zero
                ref[k, s * 64:s * 64 + 64, 128:256] = zero

    pooled = zero_sum
    for k in range(6):
        b, j = k // 2, k % 2
        if k == 0:
            spread(0)

        def keep(y, out, energy):
            zs[k, y] = out
            return energy + over_pairs(out * out)

        energy = conv(xs.at[k], wf.at[k], keep, zero_sum)
        r = lax.rsqrt(both(energy) * (1.0 / 64) + eps)
        rs[k] = r
        scale = r * twice(gain[b, j:j + 1, :])
        shift = twice(bias[b, j:j + 1, :])

        def activate(y, carry):
            u = zs[k, y].reshape(4, 64, 128) * scale[None] + shift[None]
            if j == 1:
                u = u + xs[k - 1, y + 1, :, 0:128].astype(F32).reshape(4, 64, 128)
            sig = 0.5 * jnp.tanh(0.5 * u) + 0.5
            out = u * sig
            dsw[k, y] = (sig + out * (1.0 - sig)).reshape(256, 128)
            if k < 5:
                put(xs.at[k + 1], y, out)
                return carry
            return carry + jnp.sum(out.astype(BF16).astype(F32), axis=0)

        if k < 5:
            spread(k + 1)
        pooled = lax.fori_loop(0, 8, activate, pooled, unroll=8)

    pooled = both(pooled) * (1.0 / 64)
    hw2[...] = jnp.zeros((128, 128), F32)
    hw2[0:hw.shape[0], :] = twice(hw[...])
    lab[...] = jnp.zeros((8, 128), jnp.int32)
    lab[0:1, 0:64] = labels[...]
    hbias = jnp.concatenate([hb[...], jnp.zeros((1, 128 - classes), F32)], axis=1)
    logits = dot_f32(jnp.where(low, pooled, 0.0), hw2[...].T) + hbias
    live = lane < classes
    logits = jnp.where(live, logits, -1e30)
    top = jnp.max(logits, axis=1, keepdims=True)
    expo = jnp.where(live, jnp.exp(logits - top), 0.0)
    probs = expo / jnp.sum(expo, axis=1, keepdims=True)
    onehot = jnp.where(
        lax.broadcasted_iota(jnp.int32, (128, 128), 0) == lab[0:1, :], 1.0, 0.0).T
    dl = (probs - onehot[0:64]) * (1.0 / total)
    dlt = jnp.concatenate([dl, jnp.zeros((64, 128), F32)], axis=0).T
    tall = jnp.concatenate([pooled, jnp.zeros((64, 128), F32)], axis=0)
    d_head = dot_f32(dlt[0:16], tall)
    row = lax.broadcasted_iota(jnp.int32, (8, 128), 0)
    d_bias = pltpu.roll(jnp.sum(dl, axis=0, keepdims=True), 64, 1)
    head_rows = {
        5: jnp.where(row >= 2, pltpu.roll(d_head[0:8], 2, 0), 0.0),
        4: jnp.where(row == 6, d_bias,
                     jnp.where(row >= 4, pltpu.roll(d_head[8:16], 4, 0),
                               pltpu.roll(d_head[0:8], 4, 0))),
    }
    spread_g = dot_f32(dl, hw2[...]) * (1.0 / 64)
    spread_g = spread_g.astype(BF16).astype(F32)

    def advance(k):
        for act, other in AFTER.get(k, ()):
            {"b": start_b, "f": finish}[act](other)

    def tally(k, y, d, sums):
        return (sums[0] + over_pairs(d * zs[k, y]), sums[1] + over_pairs(d))

    def begin(y, sums):
        d = (dsw[5, y].reshape(4, 64, 128) * spread_g[None]).reshape(256, 128)
        du2[y] = d
        return tally(5, y, d, sums)

    sums = lax.fori_loop(0, 8, begin, (zero_sum, zero_sum))
    for k in range(5, -1, -1):
        b, j = k // 2, k % 2
        source = du2 if j == 1 else du1
        r = rs[k]
        dg = both(sums[0]) * r
        db = both(sums[1])
        extra = jnp.where(row == 0, jnp.sum(dg, axis=0, keepdims=True),
                          jnp.where(row == 1, jnp.sum(db, axis=0, keepdims=True),
                                    head_rows.get(k, 0.0)))
        top = extra.astype(BF16).astype(F32)
        side = jnp.concatenate([top, extra - top] * secs, axis=0)
        c1 = r * twice(gain[b, j:j + 1, :])
        c2 = c1 * dg * r * (1.0 / 64)

        def settle(y, carry):
            d = (source[y].reshape(4, 64, 128) * c1[None]
                 - zs[k, y].reshape(4, 64, 128) * c2[None])
            if k > 0:
                put(qs, y, d)
            qt[y + 1] = d.reshape(256, 128).T.astype(BF16)
            return carry

        lax.fori_loop(0, 8, settle, 0, unroll=8)

        def weight_terms(*accs):
            for step in range(4):
                for m in range(2):
                    y = 2 * step + m
                    pltpu.matmul_push_rhs(xs[k, y + 1], step % 2, m)
                    for a in range(3):
                        pltpu.matmul_acc_lhs(accs[3 * m + a], qt[y - a + 2],
                                             load_staged_rhs=step % 2 if a == 0 else None)
            return jnp.concatenate(
                [pltpu.matmul_pop(accs[a]) + pltpu.matmul_pop(accs[3 + a]) for a in range(3)], axis=0)

        terms = pl.run_scoped(
            weight_terms, *[pltpu.ACC(m)((128, 256), F32) for m in range(2) for _ in range(3)])
        def rolled(a):
            return (pltpu.roll(terms[a * 128:a * 128 + 64], 64, 1)
                    + terms[a * 128 + 64:a * 128 + 128])

        first, last = rolled(0), rolled(2)
        swapped = jnp.concatenate([terms[128:192, 128:256], terms[128:192, 0:128]], axis=1)
        middle = swapped + pltpu.roll(terms[192:256], 64, 1)
        tiles = [first[:, 0:128], jnp.where(low, first[:, 128:256], middle[:, 0:128]),
                 middle[:, 128:256], last[:, 0:128], jnp.where(low, last[:, 128:256], side)]
        for m in range(TILES):
            v = tiles[m].astype(BF16)
            for q in range(secs):
                buf[k, q, m] = v[q * 16:q * 16 + 16]
        start_a(k)

        if j == 1:
            def to_first(y, out, sums):
                d = out * dsw[k - 1, y]
                du1[y] = d
                return tally(k - 1, y, d, sums)

            sums = conv(qs, wb.at[k], to_first, (zero_sum, zero_sum))
            advance(k)
        elif k > 0:
            def to_second(y, out, sums):
                g = (du2[y] + out).astype(BF16).astype(F32)
                d = g * dsw[k - 1, y]
                du2[y] = d
                return tally(k - 1, y, d, sums)

            sums = conv(qs, wb.at[k], to_second, (zero_sum, zero_sum))
            advance(k)

    for act, k in TAIL:
        {"b": start_b, "f": finish}[act](k)
    for k in range(6):
        for d in range(1, secs):
            send_w(k, d).wait_send()
    for k in range(6):
        for d in range(1, group):
            send_a(k, d).wait_send()
        each(rows_of, lambda d: send_b(k, d, line).wait_send())


def all_grads(total, dps, secs, images_in, labels, own, gain, bias, hw, hb):
    vmem = pl.BlockSpec(memory_space=pltpu.VMEM)
    hbm = pl.BlockSpec(memory_space=pltpu.HBM)
    dma = pltpu.SemaphoreType.DMA
    pair = 2 if dps % 2 == 0 else 1
    group = pair * secs
    return pl.pallas_call(
        functools.partial(kernel, total, dps, secs),
        out_shape=(jax.ShapeDtypeStruct(own.shape, F32),
                   jax.ShapeDtypeStruct(gain.shape[:2] + (2,) + gain.shape[2:], F32),
                   jax.ShapeDtypeStruct(hw.shape, F32),
                   jax.ShapeDtypeStruct(hb.shape, F32)),
        in_specs=[hbm, vmem, hbm, vmem, vmem, vmem, vmem],
        out_specs=(vmem, vmem, vmem, vmem),
        scratch_shapes=[
            pltpu.VMEM((6, 10, 256, 256), BF16),
            pltpu.VMEM((6, 8, 256, 128), F32),
            pltpu.VMEM((6, 8, 256, 128), F32),
            pltpu.VMEM((6, 64, 128), F32),
            pltpu.VMEM((6, 1024, 256), BF16),
            pltpu.VMEM((6, 1024, 256), BF16),
            pltpu.VMEM((10, 256, 256), BF16),
            pltpu.VMEM((10, 128, 256), BF16),
            pltpu.VMEM((8, 256, 128), F32),
            pltpu.VMEM((8, 256, 128), F32),
            pltpu.VMEM((128, 128), F32),
            pltpu.VMEM((8, 128), jnp.int32),
            pltpu.VMEM((secs,) + own.shape, BF16),
            pltpu.VMEM((6, secs, TILES, 16, 128), BF16),
            pltpu.VMEM((6, group, TILES, 16, 128), BF16),
            pltpu.VMEM((6, dps // pair, TILES, 16, 128), BF16),
            pltpu.VMEM(images_in.shape, BF16),
            pltpu.VMEM(own.shape, F32),
            dma((2,)),
            dma((6, secs - 1)), dma((6, secs - 1)),
            dma((6, group - 1)), dma((6, group - 1)),
            dma((6, dps // pair - 1)), dma((6, dps // pair - 1)),
        ],
        compiler_params=pltpu.CompilerParams(
            vmem_limit_bytes=63 * 1024 * 1024 + 768 * 1024, collective_id=0, has_side_effects=True),
    )(images_in, labels, own, gain, bias, hw, hb)


def hand_over(*refs):
    half = len(refs) // 2
    for i in range(half):
        refs[half + i][...] = refs[i][...]


def outputs(*arrays):
    vmem = pl.BlockSpec(memory_space=pltpu.VMEM)
    return pl.pallas_call(
        hand_over,
        out_shape=tuple(jax.ShapeDtypeStruct(v.shape, v.dtype) for v in arrays),
        in_specs=[vmem] * len(arrays),
        out_specs=(vmem,) * len(arrays),
    )(*arrays)


def per_device(images_in, labels, conv_weight, frn_gain, frn_bias, head_weight, head_bias):
    images = images_in.shape[0]
    dps, secs = lax.axis_size("dp"), lax.axis_size("section")
    blocks, convs, depth, share = conv_weight.shape
    own = jnp.swapaxes(conv_weight, 2, 3).reshape(blocks * convs, share, depth)
    conv, norm, head, head_b = outputs(*all_grads(
        images * dps * secs, dps, secs, images_in, labels.reshape(1, images), own, frn_gain,
        frn_bias, head_weight.T, head_bias.reshape(1, -1)))
    return (jnp.swapaxes(conv.reshape(blocks, convs, share, depth), 2, 3), norm, head.T,
            head_b.reshape(-1))


def solution(mesh):
    return jax.shard_map(
        per_device,
        mesh=mesh,
        in_specs=(
            P(("dp", "section"), None),
            P(("dp", "section")),
            P(None, None, None, "section"),
            P(),
            P(),
            P(),
            P(),
        ),
        out_specs=(P(None, None, None, "section"), P(), P(), P()),
        check_vma=False,
    )
```

```python
import functools

import jax
import jax.numpy as jnp
from jax import lax
from jax.experimental import pallas as pl
from jax.experimental.pallas import tpu as pltpu
from jax.sharding import PartitionSpec as P

F32 = jnp.float32
BF16 = jnp.bfloat16
MESH = pl.DeviceIdType.MESH
eps = 1e-06
prior_precision = 0.5
OFFSETS = (0, 1, 2, -1)


TILES = 5
AFTER = {3: (("b", 5),), 2: (("b", 4),), 1: (("b", 3),)}
TAIL = (("b", 2), ("b", 1), ("f", 5), ("b", 0), ("f", 4), ("f", 3), ("f", 2), ("f", 1))


def kernel(total, dps, secs, img_hbm, labels, own_hbm, gain, bias, hw, hb,
           conv_out, norm_out, hw_out, hb_out,
           xs, zs, dsw, rs, wf, wb, qs, qt, du2, du1, hw2, lab, wt, buf, in_a, in_b, img, own, load, w_send, w_recv, a_send, a_recv, b_send, b_recv):
    dp, sec = lax.axis_index("dp"), lax.axis_index("section")
    lane = lax.broadcasted_iota(jnp.int32, (1, 128), 1)
    low = lane < 64
    classes = hw.shape[0]
    pair = 2 if dps % 2 == 0 else 1
    group, rows_of = pair * secs, dps // pair
    line, side_of = dp // pair, lax.rem(dp, pair)
    mine = side_of * secs + sec

    def each(n, act):
        def step(d, carry):
            act(d)
            return carry
        lax.fori_loop(1, n, step, 0)

    load_own = pltpu.make_async_copy(own_hbm, own, load.at[0])
    load_img = pltpu.make_async_copy(img_hbm, img, load.at[1])
    load_own.start()
    load_img.start()
    barrier = pltpu.get_barrier_semaphore()
    for d in range(1, group):
        to = lax.rem(mine + d, group)
        pl.semaphore_signal(barrier, inc=1,
                            device_id=(line * pair + to // secs, lax.rem(to, secs)),
                            device_id_type=MESH)
    each(rows_of, lambda d: pl.semaphore_signal(
        barrier, inc=1, device_id=(lax.rem(line + d, rows_of) * pair + side_of, sec),
        device_id_type=MESH))
    load_own.wait()
    wt[sec] = own[...].astype(BF16)
    pl.semaphore_wait(barrier, group - 1 + rows_of - 1)

    def send_w(k, d):
        mine = wt.at[sec, k]
        return pltpu.make_async_remote_copy(
            src_ref=mine, dst_ref=mine, send_sem=w_send.at[k, d - 1],
            recv_sem=w_recv.at[k, d - 1], device_id=(dp, lax.rem(sec + d, secs)),
            device_id_type=MESH)

    def send_a(k, d):
        to = lax.rem(mine + d, group)
        return pltpu.make_async_remote_copy(
            src_ref=buf.at[k, lax.rem(to, secs)], dst_ref=in_a.at[k, mine],
            send_sem=a_send.at[k, d - 1], recv_sem=a_recv.at[k, d - 1],
            device_id=(line * pair + to // secs, lax.rem(to, secs)), device_id_type=MESH)

    def wait_a(k, d):
        to = lax.rem(mine + d, group)
        pltpu.make_async_remote_copy(
            src_ref=buf.at[k, lax.rem(to, secs)], dst_ref=in_a.at[k, lax.rem(mine + group - d, group)],
            send_sem=a_send.at[k, d - 1], recv_sem=a_recv.at[k, d - 1],
            device_id=(line * pair + to // secs, lax.rem(to, secs)),
            device_id_type=MESH).wait_recv()

    def send_b(k, d, slot):
        to = lax.rem(line + d, rows_of)
        return pltpu.make_async_remote_copy(
            src_ref=in_b.at[k, line], dst_ref=in_b.at[k, slot], send_sem=b_send.at[k, d - 1],
            recv_sem=b_recv.at[k, d - 1], device_id=(to * pair + side_of, sec),
            device_id_type=MESH)

    def resplit(v):
        whole = v[0:8] + v[8:16]
        top = whole.astype(BF16).astype(F32)
        return jnp.where(low, v, jnp.concatenate([top, whole - top], axis=0))

    def start_a(k):
        for d in range(1, group):
            send_a(k, d).start()
        in_a[k, mine] = buf[k, sec]

    def add_up(ref, k, m, n):
        v = ref[k, 0, m].astype(F32)
        if n <= 8:
            for p in range(1, n):
                v = v + ref[k, p, m].astype(F32)
            return v
        return lax.fori_loop(1, n, lambda p, acc: acc + ref[k, p, m].astype(F32), v)

    def start_b(k):
        for d in range(1, group):
            wait_a(k, d)
        for m in range(TILES):
            v = add_up(in_a, k, m, group)
            in_b[k, line, m] = (resplit(v) if m == TILES - 1 else v).astype(BF16)
        each(rows_of, lambda d: send_b(k, d, line).start())

    def finish(k):
        each(rows_of, lambda d: send_b(k, d, lax.rem(line + rows_of - d, rows_of)).wait_recv())
        rows = [add_up(in_b, k, m, rows_of) for m in range(TILES)]
        side = pltpu.roll(rows[-1][0:8] + rows[-1][8:16], 64, 1)[:, 0:64]
        conv_out[k] = (jnp.concatenate(rows[:-1] + [rows[-1][:, 0:64]], axis=1)
                       + prior_precision * own[k])
        b, j = k // 2, k % 2
        norm_out[b, j, 0:1] = side[0:1] + prior_precision * gain[b, j:j + 1, :]
        norm_out[b, j, 1:2] = side[1:2] + prior_precision * bias[b, j:j + 1, :]
        if k == 5:
            hw_out[0:6] = side[2:8] + prior_precision * hw[0:6]
        if k == 4:
            hw_out[6:classes] = side[2:classes - 4] + prior_precision * hw[6:classes]
            hb_out[...] = side[6:7, 0:classes] + prior_precision * hb[...]

    for k in range(6):
        for d in range(1, secs):
            send_w(k, d).start()

    def both(v):
        return v + pltpu.roll(v, 64, 1)

    def twice(v):
        return jnp.concatenate([v, v], axis=1)

    for ref in (qs, qt):
        ref[0] = jnp.zeros(ref.shape[1:], BF16)
        ref[9] = jnp.zeros(ref.shape[1:], BF16)
    for k in range(6):
        xs[k, 0] = jnp.zeros((256, 256), BF16)
        xs[k, 9] = jnp.zeros((256, 256), BF16)

    def put(ref, y, v):
        edge = jnp.zeros((1, 64, 128), F32)
        after = jnp.concatenate([v[1:], edge], axis=0)
        before = jnp.concatenate([edge, v[:3]], axis=0)
        beside = jnp.where(low[None], after, before)
        ref[y + 1, :, 0:128] = v.reshape(256, 128).astype(BF16)
        ref[y + 1, :, 128:256] = beside.reshape(256, 128).astype(BF16)

    def conv(src, w, body, init):
        def run(*accs):
            for m in range(2):
                for kt in range(2):
                    at = (2 * m + kt) * 256
                    pltpu.matmul_push_rhs(w[at:at + 256, :], kt, m)
            for kt in range(2):
                for y2 in range(4):
                    for m in range(2):
                        pltpu.matmul_acc_lhs(accs[4 * m + y2], src[2 * y2 + 2 * m + kt],
                                             load_staged_rhs=kt if y2 == 0 else None)
            carry = init
            for y2 in range(4):
                out = pltpu.matmul_pop(accs[y2]) + pltpu.matmul_pop(accs[4 + y2])
                for yo in range(2):
                    carry = body(2 * y2 + yo, out[:, yo * 128:yo * 128 + 128], carry)
            return carry

        return pl.run_scoped(run, *[pltpu.ACC(m)((256, 256), F32) for m in range(2) for _ in range(4)])

    def split(v):
        top = v.astype(BF16)
        return [top, (v - top.astype(F32)).astype(BF16)]

    def dot_f32(a, b):
        def run(acc):
            half = jnp.concatenate(split(b), axis=1)
            pltpu.matmul_push_rhs(jnp.concatenate([half, half], axis=0), 0, 0)
            pltpu.matmul_acc_lhs(acc, jnp.concatenate(split(a), axis=1), load_staged_rhs=0)
            out = pltpu.matmul_pop(acc)
            return out[:, 0:128] + out[:, 128:256]

        return pl.run_scoped(run, pltpu.ACC(0)((a.shape[0], 256), F32))

    zero_sum = jnp.zeros((64, 128), F32)

    def over_pairs(v):
        return jnp.sum(v.reshape(4, 64, 128), axis=0)

    load_img.wait()
    for y in range(8):
        slab = jnp.stack([img[:, (y * 4 + j) * 128:(y * 4 + j + 1) * 128]
                          for j in range(4)], axis=0).astype(F32)
        put(xs.at[0], y, slab)

    def spread(k):
        b, j = k // 2, k % 2
        for d in range(1, secs):
            send_w(k, d).wait_recv()
        zero = jnp.zeros((64, 128), BF16)
        none = jnp.zeros((64, 128), F32)
        flat = jnp.concatenate([wt[q, k] for q in range(secs)], axis=0).astype(F32)
        wide = jnp.concatenate([none[:, 0:64], flat, none], axis=1)
        square = jnp.concatenate([flat, none[:, 0:64]], axis=1)
        cols = jnp.concatenate([square, square], axis=0).T
        plain = [cols[t * 64:(t + 1) * 64] for t in range(9)]
        for a in range(3):
            for s, xi in enumerate(OFFSETS):
                left = plain[a * 3 + xi + 1] if 0 <= xi + 1 <= 2 else none
                right = plain[a * 3 + xi] if 0 <= xi <= 2 else none
                tile = jnp.where(low, left, right).astype(BF16)
                at = ((2 - a) * 3 + 2 - xi) * 64
                back = wide[:, at:at + 128]
                if xi == -1:
                    back = jnp.where(low, back, 0.0)
                if xi == 2:
                    back = jnp.where(low, 0.0, back)
                back = back.astype(BF16)
                for yo in range(2):
                    row = (a + yo) * 256 + s * 64
                    wf[k, row:row + 64, yo * 128:yo * 128 + 128] = tile
                    if k > 0:
                        wb[k, row:row + 64, yo * 128:yo * 128 + 128] = back
        for ref in (wf, wb):
            for s in range(4):
                ref[k, 768 + s * 64:832 + s * 64, 0:128] = zero
                ref[k, s * 64:s * 64 + 64, 128:256] = zero

    pooled = zero_sum
    for k in range(6):
        b, j = k // 2, k % 2
        if k == 0:
            spread(0)

        def keep(y, out, energy):
            zs[k, y] = out
            return energy + over_pairs(out * out)

        energy = conv(xs.at[k], wf.at[k], keep, zero_sum)
        r = lax.rsqrt(both(energy) * (1.0 / 64) + eps)
        rs[k] = r
        scale = r * twice(gain[b, j:j + 1, :])
        shift = twice(bias[b, j:j + 1, :])

        def activate(y, carry):
            u = zs[k, y].reshape(4, 64, 128) * scale[None] + shift[None]
            if j == 1:
                u = u + xs[k - 1, y + 1, :, 0:128].astype(F32).reshape(4, 64, 128)
            sig = 0.5 * jnp.tanh(0.5 * u) + 0.5
            out = u * sig
            dsw[k, y] = (sig + out * (1.0 - sig)).reshape(256, 128)
            if k < 5:
                put(xs.at[k + 1], y, out)
                return carry
            return carry + jnp.sum(out.astype(BF16).astype(F32), axis=0)

        if k < 5:
            spread(k + 1)
        pooled = lax.fori_loop(0, 8, activate, pooled, unroll=8)

    pooled = both(pooled) * (1.0 / 64)
    hw2[...] = jnp.zeros((128, 128), F32)
    hw2[0:hw.shape[0], :] = twice(hw[...])
    lab[...] = jnp.zeros((8, 128), jnp.int32)
    lab[0:1, 0:64] = labels[...]
    hbias = jnp.concatenate([hb[...], jnp.zeros((1, 128 - classes), F32)], axis=1)
    logits = dot_f32(jnp.where(low, pooled, 0.0), hw2[...].T) + hbias
    live = lane < classes
    logits = jnp.where(live, logits, -1e30)
    top = jnp.max(logits, axis=1, keepdims=True)
    expo = jnp.where(live, jnp.exp(logits - top), 0.0)
    probs = expo / jnp.sum(expo, axis=1, keepdims=True)
    onehot = jnp.where(
        lax.broadcasted_iota(jnp.int32, (128, 128), 0) == lab[0:1, :], 1.0, 0.0).T
    dl = (probs - onehot[0:64]) * (1.0 / total)
    dlt = jnp.concatenate([dl, jnp.zeros((64, 128), F32)], axis=0).T
    tall = jnp.concatenate([pooled, jnp.zeros((64, 128), F32)], axis=0)
    d_head = dot_f32(dlt[0:16], tall)
    row = lax.broadcasted_iota(jnp.int32, (8, 128), 0)
    d_bias = pltpu.roll(jnp.sum(dl, axis=0, keepdims=True), 64, 1)
    head_rows = {
        5: jnp.where(row >= 2, pltpu.roll(d_head[0:8], 2, 0), 0.0),
        4: jnp.where(row == 6, d_bias,
                     jnp.where(row >= 4, pltpu.roll(d_head[8:16], 4, 0),
                               pltpu.roll(d_head[0:8], 4, 0))),
    }
    spread_g = dot_f32(dl, hw2[...]) * (1.0 / 64)
    spread_g = spread_g.astype(BF16).astype(F32)

    def advance(k):
        for act, other in AFTER.get(k, ()):
            {"b": start_b, "f": finish}[act](other)

    def tally(k, y, d, sums):
        return (sums[0] + over_pairs(d * zs[k, y]), sums[1] + over_pairs(d))

    def begin(y, sums):
        d = (dsw[5, y].reshape(4, 64, 128) * spread_g[None]).reshape(256, 128)
        du2[y] = d
        return tally(5, y, d, sums)

    sums = lax.fori_loop(0, 8, begin, (zero_sum, zero_sum))
    for k in range(5, -1, -1):
        b, j = k // 2, k % 2
        source = du2 if j == 1 else du1
        r = rs[k]
        dg = both(sums[0]) * r
        db = both(sums[1])
        extra = jnp.where(row == 0, jnp.sum(dg, axis=0, keepdims=True),
                          jnp.where(row == 1, jnp.sum(db, axis=0, keepdims=True),
                                    head_rows.get(k, 0.0)))
        top = extra.astype(BF16).astype(F32)
        side = jnp.concatenate([top, extra - top] * secs, axis=0)
        c1 = r * twice(gain[b, j:j + 1, :])
        c2 = c1 * dg * r * (1.0 / 64)

        def settle(y, carry):
            d = (source[y].reshape(4, 64, 128) * c1[None]
                 - zs[k, y].reshape(4, 64, 128) * c2[None])
            if k > 0:
                put(qs, y, d)
            qt[y + 1] = d.reshape(256, 128).T.astype(BF16)
            return carry

        lax.fori_loop(0, 8, settle, 0, unroll=8)

        def weight_terms(*accs):
            for step in range(4):
                for m in range(2):
                    y = 2 * step + m
                    pltpu.matmul_push_rhs(xs[k, y + 1], step % 2, m)
                    for a in range(3):
                        pltpu.matmul_acc_lhs(accs[3 * m + a], qt[y - a + 2],
                                             load_staged_rhs=step % 2 if a == 0 else None)
            return jnp.concatenate(
                [pltpu.matmul_pop(accs[a]) + pltpu.matmul_pop(accs[3 + a]) for a in range(3)], axis=0)

        terms = pl.run_scoped(
            weight_terms, *[pltpu.ACC(m)((128, 256), F32) for m in range(2) for _ in range(3)])
        def rolled(a):
            return (pltpu.roll(terms[a * 128:a * 128 + 64], 64, 1)
                    + terms[a * 128 + 64:a * 128 + 128])

        first, last = rolled(0), rolled(2)
        swapped = jnp.concatenate([terms[128:192, 128:256], terms[128:192, 0:128]], axis=1)
        middle = swapped + pltpu.roll(terms[192:256], 64, 1)
        tiles = [first[:, 0:128], jnp.where(low, first[:, 128:256], middle[:, 0:128]),
                 middle[:, 128:256], last[:, 0:128], jnp.where(low, last[:, 128:256], side)]
        for m in range(TILES):
            v = tiles[m].astype(BF16)
            for q in range(secs):
                buf[k, q, m] = v[q * 16:q * 16 + 16]
        start_a(k)

        if j == 1:
            def to_first(y, out, sums):
                d = out * dsw[k - 1, y]
                du1[y] = d
                return tally(k - 1, y, d, sums)

            sums = conv(qs, wb.at[k], to_first, (zero_sum, zero_sum))
            advance(k)
        elif k > 0:
            def to_second(y, out, sums):
                g = (du2[y] + out).astype(BF16).astype(F32)
                d = g * dsw[k - 1, y]
                du2[y] = d
                return tally(k - 1, y, d, sums)

            sums = conv(qs, wb.at[k], to_second, (zero_sum, zero_sum))
            advance(k)

    for act, k in TAIL:
        {"b": start_b, "f": finish}[act](k)
    for k in range(6):
        for d in range(1, secs):
            send_w(k, d).wait_send()
        for d in range(1, group):
            send_a(k, d).wait_send()
        if k > 0:
            each(rows_of, lambda d: send_b(k, d, line).wait_send())
    finish(0)
    each(rows_of, lambda d: send_b(0, d, line).wait_send())


def all_grads(total, dps, secs, images_in, labels, own, gain, bias, hw, hb):
    vmem = pl.BlockSpec(memory_space=pltpu.VMEM)
    hbm = pl.BlockSpec(memory_space=pltpu.HBM)
    dma = pltpu.SemaphoreType.DMA
    pair = 2 if dps % 2 == 0 else 1
    group = pair * secs
    return pl.pallas_call(
        functools.partial(kernel, total, dps, secs),
        out_shape=(jax.ShapeDtypeStruct(own.shape, F32),
                   jax.ShapeDtypeStruct(gain.shape[:2] + (2,) + gain.shape[2:], F32),
                   jax.ShapeDtypeStruct(hw.shape, F32),
                   jax.ShapeDtypeStruct(hb.shape, F32)),
        in_specs=[hbm, vmem, hbm, vmem, vmem, vmem, vmem],
        out_specs=(vmem, vmem, vmem, vmem),
        scratch_shapes=[
            pltpu.VMEM((6, 10, 256, 256), BF16),
            pltpu.VMEM((6, 8, 256, 128), F32),
            pltpu.VMEM((6, 8, 256, 128), F32),
            pltpu.VMEM((6, 64, 128), F32),
            pltpu.VMEM((6, 1024, 256), BF16),
            pltpu.VMEM((6, 1024, 256), BF16),
            pltpu.VMEM((10, 256, 256), BF16),
            pltpu.VMEM((10, 128, 256), BF16),
            pltpu.VMEM((8, 256, 128), F32),
            pltpu.VMEM((8, 256, 128), F32),
            pltpu.VMEM((128, 128), F32),
            pltpu.VMEM((8, 128), jnp.int32),
            pltpu.VMEM((secs,) + own.shape, BF16),
            pltpu.VMEM((6, secs, TILES, 16, 128), BF16),
            pltpu.VMEM((6, group, TILES, 16, 128), BF16),
            pltpu.VMEM((6, dps // pair, TILES, 16, 128), BF16),
            pltpu.VMEM(images_in.shape, BF16),
            pltpu.VMEM(own.shape, F32),
            dma((2,)),
            dma((6, secs - 1)), dma((6, secs - 1)),
            dma((6, group - 1)), dma((6, group - 1)),
            dma((6, dps // pair - 1)), dma((6, dps // pair - 1)),
        ],
        compiler_params=pltpu.CompilerParams(
            vmem_limit_bytes=63 * 1024 * 1024 + 768 * 1024, collective_id=0, has_side_effects=True),
    )(images_in, labels, own, gain, bias, hw, hb)


def hand_over(*refs):
    half = len(refs) // 2
    for i in range(half):
        refs[half + i][...] = refs[i][...]


def outputs(*arrays):
    vmem = pl.BlockSpec(memory_space=pltpu.VMEM)
    return pl.pallas_call(
        hand_over,
        out_shape=tuple(jax.ShapeDtypeStruct(v.shape, v.dtype) for v in arrays),
        in_specs=[vmem] * len(arrays),
        out_specs=(vmem,) * len(arrays),
    )(*arrays)


def per_device(images_in, labels, conv_weight, frn_gain, frn_bias, head_weight, head_bias):
    images = images_in.shape[0]
    dps, secs = lax.axis_size("dp"), lax.axis_size("section")
    blocks, convs, depth, share = conv_weight.shape
    own = jnp.swapaxes(conv_weight, 2, 3).reshape(blocks * convs, share, depth)
    conv, norm, head, head_b = outputs(*all_grads(
        images * dps * secs, dps, secs, images_in, labels.reshape(1, images), own, frn_gain,
        frn_bias, head_weight.T, head_bias.reshape(1, -1)))
    return (jnp.swapaxes(conv.reshape(blocks, convs, share, depth), 2, 3), norm, head.T,
            head_b.reshape(-1))


def solution(mesh):
    return jax.shard_map(
        per_device,
        mesh=mesh,
        in_specs=(
            P(("dp", "section"), None),
            P(("dp", "section")),
            P(None, None, None, "section"),
            P(),
            P(),
            P(),
            P(),
        ),
        out_specs=(P(None, None, None, "section"), P(), P(), P()),
        check_vma=False,
    )
```
